32 devices in a mesh: groups: 2 (over x), kv: 16 (over z, y, core).
Axes of the slice: x: 2, y: 2, z: 4, core: 2. Of those that a mesh axis runs over, the one named last changes fastest.
Arguments:
- query_in: bfloat16 [256, 2048], P(('groups', 'kv')), parts along dimension 0, may hold values from -6 to 6
- key_in: bfloat16 [256, 512], P(('groups', 'kv')), parts along dimension 0, may hold values from -16 to 16
- value_in: bfloat16 [256, 512], P(('groups', 'kv')), parts along dimension 0, may hold values from -6 to 6
- cache_keys: bfloat16 [4, 6144, 512], P('groups', 'kv'), parts along dimension 0, may hold values from -700 to 700
- cache_values: bfloat16 [4, 6144, 512], P('groups', 'kv'), parts along dimension 0, may hold values from -6 to 6
- live_slots: int32 [4, 16], P('groups', 'kv'), parts along dimension 0, may hold values from 0 to 384, as said below
- span_starts: int32 [4], P('groups'), parts along dimension 0, may hold values from 0 to 1048447
Outputs:
- attended: bfloat16 [256, 2048], P(('groups', 'kv')), parts along dimension 0
The draws below stay inside these ranges and needn't reach their ends.
There are 2 independent parts, one for each index of `groups`. The reference program is written for one: setup_inputs(seed, part) draws one part's arguments, and reference() takes and returns one part's arrays. A program takes and returns all parts, laid end to end along the dimension named above; each array names one. Nothing has to cross between parts.
Inputs may be any that keep to these rules, and one draw needn't show every extreme that they name: `live_slots`: in every block some device has all 384 of its slots live.
All inputs are finite; a program needn't handle non-finite values.
Results may differ from the reference program's by a relative error of at most 0.006.
The reference program's roundings to bfloat16 on the way count: a program that leaves them out, or rounds other values in their place, can miss the bound.
Values may be sent and summed in bfloat16 or wider, within the bound.
A program may use at most 320 MiB of HBM per device.

```python
import jax
import jax.numpy as jnp
import numpy as np
from jax import lax

H = 16
KVH = 4
HD = 128
CH = 64
SPANS = 2
SLOT_DEV = 384
TOK = 128
SLOTS = 6144
N_KV = 16


def draw_cache_keys(key, part):
    base_draw = 3.5 * jax.random.normal(jax.random.fold_in(key, 11), (SPANS, SLOTS, KVH * HD), jnp.float32)
    return jnp.clip(base_draw, -700.0, 700.0).astype(jnp.bfloat16)


def draw_live_slots(key, part):
    shard_count = SLOTS // SLOT_DEV
    live_counts = jax.random.randint(jax.random.fold_in(key, 21), (SPANS, shard_count), 0, SLOT_DEV + 1)
    full_shard = jax.random.randint(jax.random.fold_in(key, 22), (SPANS,), 0, shard_count)
    filled = jnp.arange(shard_count)[None, :] == full_shard[:, None]
    return jnp.where(filled, SLOT_DEV, live_counts).astype(jnp.int32)


def block_levels(key, dims, cuts, low, top_value):
    level, own = 1.0, jax.random.fold_in(key, 6)
    for dim, parts in cuts:
        heights = jnp.exp(jax.random.uniform(jax.random.fold_in(own, dim), (parts,), jnp.float32, low / len(cuts), top_value / len(cuts)))
        level = level * jnp.repeat(heights, dims[dim] // parts).reshape([-1 if axis == dim else 1 for axis in range(len(dims))])
    return level


def gaussian(rng, dims, spread, limit, split=(), held_as=jnp.bfloat16):
    array = jax.random.normal(rng, dims, jnp.float32) * spread
    if len(split) > 0:
        array = block_levels(rng, dims, split, -0.22, 0.18) * array
    return jnp.clip(array, min=-limit, max=limit).astype(held_as)


def setup_inputs(seed: int = 0, part: int = 0) -> dict:
    splits = jax.random.split(jax.random.key(seed), 8)
    part_keys = jax.random.split(jax.random.fold_in(splits[7], part), 8)
    query_in = gaussian(part_keys[0], (TOK, H * HD), 1.0, 6.0, ((0, 16),))
    key_in = gaussian(part_keys[1], (TOK, KVH * HD), 3.5, 16.0, ((0, 16),))
    value_in = gaussian(part_keys[2], (TOK, KVH * HD), 1.0, 6.0, ((0, 16),))
    cache_keys = draw_cache_keys(jax.random.fold_in(jax.random.fold_in(splits[7], part), 71), part)
    cache_values = gaussian(part_keys[4], (SPANS, SLOTS, KVH * HD), 1.0, 6.0, ((1, 16),))
    live_slots = draw_live_slots(jax.random.fold_in(jax.random.fold_in(splits[7], part), 71), part)
    span_starts = jax.random.randint(part_keys[6], (SPANS,), 0, 1048448).astype(jnp.int32)
    return dict(query_in=query_in, key_in=key_in, value_in=value_in, cache_keys=cache_keys, cache_values=cache_values, live_slots=live_slots, span_starts=span_starts)


NEG_FILL = -1e30


def turn_table(head_size):
    half_size = head_size // 2
    frequency = 500000.0 ** (-np.arange(half_size) * 2.0 / head_size)
    turn_counts = np.floor(frequency / (2.0 * np.pi) * 2.0 ** 32 + 0.5).astype(np.int64) % (2 ** 32)
    turn_counts = np.where(turn_counts >= 2 ** 31, turn_counts - 2 ** 32, turn_counts)
    return jnp.asarray(turn_counts.astype(np.int32))


def rotate_pairs(values, positions):
    half_size = values.shape[-1] // 2
    phases = positions[:, None] * turn_table(values.shape[-1])[None, :]
    angles = phases.astype(jnp.float32) * (2.0 * np.pi / 2.0 ** 32)
    cosine = jnp.cos(angles)[:, None, :]
    sine_table = jnp.sin(angles)[:, None, :]
    first_half = values[..., :half_size]
    second_half = values[..., half_size:]
    return jnp.concatenate([first_half * cosine - second_half * sine_table, second_half * cosine + first_half * sine_table], axis=-1)


def settle(values):
    return lax.optimization_barrier(values.astype(jnp.bfloat16)).astype(jnp.float32)


def reference(query_in, key_in, value_in, cache_keys, cache_values, live_slots, span_starts):
    tokens = SPANS * CH
    group_size = H // KVH
    score_scale = HD ** -0.5
    positions = (span_starts[:, None] + jnp.arange(CH, dtype=jnp.int32)[None, :]).reshape(tokens).astype(jnp.int32)
    queries = rotate_pairs(query_in.astype(jnp.float32).reshape(tokens, H, HD), positions).astype(jnp.bfloat16)
    keys_new = rotate_pairs(key_in.astype(jnp.float32).reshape(tokens, KVH, HD), positions).astype(jnp.bfloat16)
    values_new = value_in.reshape(tokens, KVH, HD)
    slot_index = jnp.arange(SLOT_DEV, dtype=jnp.int32)
    results = []
    for span_index in range(SPANS):
        first_row = span_index * CH
        grouped = queries[first_row:first_row + CH].reshape(CH, KVH, group_size, HD).astype(jnp.float32)
        own_keys = keys_new[first_row:first_row + CH].astype(jnp.float32)
        own_values = values_new[first_row:first_row + CH].astype(jnp.float32)
        causal = jnp.arange(CH)[:, None] >= jnp.arange(CH)[None, :]
        own_scores = jnp.einsum('rkgd,skd->kgrs', grouped, own_keys) * score_scale
        own_scores = jnp.where(causal, own_scores, NEG_FILL)
        shard_keys = cache_keys[span_index].reshape(N_KV, SLOT_DEV, KVH, HD)
        shard_values = cache_values[span_index].reshape(N_KV, SLOT_DEV, KVH, HD)
        shard_live = live_slots[span_index]

        def shard_scores(block_keys, live_count):
            scores = jnp.einsum('rkgd,skd->kgrs', grouped, block_keys.astype(jnp.float32)) * score_scale
            allowed = slot_index < live_count
            return jnp.where(allowed, scores, NEG_FILL), allowed

        def shard_max(inputs):
            scores, allowed = shard_scores(inputs[0], inputs[1])
            return jnp.max(scores, axis=-1)

        maxima = lax.map(shard_max, (shard_keys, shard_live))
        row_max = jnp.maximum(jnp.max(maxima, axis=0), jnp.max(own_scores, axis=-1))

        def add_shard(carried, inputs):
            running_total, weighted_sum = carried
            scores, allowed = shard_scores(inputs[0], inputs[2])
            weights = jnp.where(allowed, jnp.exp(scores - row_max[..., None]), 0.0)
            weighted_sum = weighted_sum + jnp.einsum('kgrs,skd->rkgd', settle(weights), inputs[1].astype(jnp.float32))
            return (running_total + jnp.sum(weights, axis=-1), weighted_sum), None

        own_weights = jnp.where(causal, jnp.exp(own_scores - row_max[..., None]), 0.0)
        initial = (jnp.sum(own_weights, axis=-1), jnp.einsum('kgrs,skd->rkgd', settle(own_weights), own_values))
        (running_total, weighted_sum), unused_out = lax.scan(add_shard, initial, (shard_keys, shard_values, shard_live))
        attended = weighted_sum / jnp.transpose(running_total, (2, 0, 1))[..., None]
        results.append(attended.reshape(CH, H * HD))
    return jnp.concatenate(results, axis=0).astype(jnp.bfloat16)
```

```python
import functools
import math

import jax
import jax.numpy as jnp
import numpy as np
from jax import lax
from jax.experimental import pallas as pl
from jax.experimental.pallas import tpu as pltpu
from jax.sharding import PartitionSpec as P

HD = 128


NEG_FILL = -1e30
NEG_FLOOR = -1e29
MESH = pl.DeviceIdType.MESH


def turn_table(head_size):
    half_size = head_size // 2
    frequency = 500000.0 ** (-np.arange(half_size) * 2.0 / head_size)
    turn_counts = np.floor(frequency / (2.0 * np.pi) * 2.0**32 + 0.5).astype(np.int64) % 2**32
    turn_counts = np.where(turn_counts >= 2**31, turn_counts - 2**32, turn_counts)
    return jnp.asarray(turn_counts.astype(np.int32))


def rotate_pairs(values, positions):
    half_size = values.shape[-1] // 2
    phases = positions[:, None] * turn_table(values.shape[-1])[None, :]
    angles = phases.astype(jnp.float32) * (2.0 * np.pi / 2.0**32)
    cosine = jnp.cos(angles)[:, None, :]
    sine_table = jnp.sin(angles)[:, None, :]
    first_half = values[..., :half_size]
    second_half = values[..., half_size:]
    return jnp.concatenate(
        [
            first_half * cosine - second_half * sine_table,
            second_half * cosine + first_half * sine_table,
        ],
        axis=-1,
    )


def partial_block(query_rows, block_keys, block_values, allowed):
    row_count = query_rows.shape[0]
    kv_heads = block_keys.shape[1]
    head_size = block_keys.shape[2]
    grouped = query_rows.reshape(row_count, kv_heads, -1, head_size)
    scores = jnp.einsum(
        "rkgd,skd->kgrs", grouped, block_keys, preferred_element_type=jnp.float32
    ) * head_size ** (-0.5)
    scores = jnp.where(allowed, scores, NEG_FILL)
    maxima = jnp.max(scores, axis=-1)
    weights = jnp.where(allowed, jnp.exp(scores - maxima[..., None]), 0.0)
    totals = jnp.sum(weights, axis=-1)
    weighted_sum = jnp.einsum(
        "kgrs,skd->rkgd",
        weights.astype(jnp.bfloat16),
        block_values,
        preferred_element_type=jnp.float32,
    )
    return (
        jnp.transpose(maxima, (2, 0, 1)).reshape(row_count, -1),
        jnp.transpose(totals, (2, 0, 1)).reshape(row_count, -1),
        weighted_sum.reshape(row_count, -1),
    )


def fold_pair(first_terms, second_terms):
    first_max, first_total, first_sum = first_terms
    second_max, second_total, second_sum = second_terms
    joint_max = jnp.maximum(first_max, second_max)
    first_factor = jnp.exp(first_max - joint_max)
    second_factor = jnp.exp(second_max - joint_max)
    row_count, head_count = joint_max.shape
    weighted = (
        first_sum.reshape(row_count, head_count, -1) * first_factor[..., None]
        + second_sum.reshape(row_count, head_count, -1) * second_factor[..., None]
    )
    return (
        joint_max,
        first_total * first_factor + second_total * second_factor,
        weighted.reshape(row_count, -1),
    )


def rescale(local_max, local_total, local_sum, global_max):
    factor = jnp.exp(local_max - global_max)
    row_count, head_count = factor.shape
    scaled_sum = (local_sum.reshape(row_count, head_count, -1) * factor[..., None]).reshape(
        row_count, -1
    )
    return (local_total * factor, scaled_sum)


def normalize(combined):
    unused_max, totals, sums = combined
    row_count, head_count = totals.shape
    return (
        (sums.reshape(row_count, head_count, -1) / totals[..., None])
        .reshape(row_count, -1)
        .astype(jnp.bfloat16)
    )


def attend_own(query_rows, row_start, keys_new, values_new, span_len):
    query_count = query_rows.shape[0]
    rows_each = min(query_count, span_len)
    blocks = max(query_count // span_len, 1)
    pieces = []
    for block_index in range(blocks):
        first_row = row_start + block_index * rows_each
        key_start = first_row // span_len * span_len
        block_keys = lax.dynamic_slice_in_dim(keys_new, key_start, span_len, 0)
        block_values = lax.dynamic_slice_in_dim(values_new, key_start, span_len, 0)
        allowed = (
            first_row - key_start + jnp.arange(rows_each)[:, None] >= jnp.arange(span_len)[None, :]
        )
        block_rows = query_rows[block_index * rows_each : (block_index + 1) * rows_each]
        pieces.append(partial_block(block_rows, block_keys, block_values, allowed))
    return tuple(
        (
            jnp.concatenate([block_terms[member] for block_terms in pieces], axis=0)
            for member in range(3)
        )
    )


def per_device(query_in, key_in, value_in, cache_keys, cache_values, live_slots, span_starts):
    devices = lax.axis_size("kv")
    device_index = lax.axis_index("kv")
    share_rows = query_in.shape[0]
    token_count = share_rows * devices
    span_count = span_starts.shape[0]
    span_len = token_count // span_count
    head_size = HD
    head_count = query_in.shape[1] // head_size
    kv_heads = key_in.shape[1] // head_size
    row_start = device_index * share_rows
    positions = (span_starts[:, None] + jnp.arange(span_len, dtype=jnp.int32)[None, :]).reshape(
        token_count
    )
    full_query, full_key, full_value = (
        lax.all_gather(query_in, "kv", axis=0, tiled=True),
        lax.all_gather(key_in, "kv", axis=0, tiled=True),
        lax.all_gather(value_in, "kv", axis=0, tiled=True),
    )
    queries = rotate_pairs(
        full_query.astype(jnp.float32).reshape(token_count, head_count, head_size), positions
    ).astype(jnp.bfloat16)
    keys_new = rotate_pairs(
        full_key.astype(jnp.float32).reshape(token_count, kv_heads, head_size), positions
    ).astype(jnp.bfloat16)
    values_new = full_value.reshape(token_count, kv_heads, head_size)
    slot_count = cache_keys.shape[1]
    slot_index = jnp.arange(slot_count)
    partials = []
    for span_index in range(span_count):
        query_rows = queries[span_index * span_len : (span_index + 1) * span_len]
        allowed = (slot_index < live_slots[span_index, 0])[None, :]
        block_keys = cache_keys[span_index].reshape(slot_count, kv_heads, head_size)
        block_values = cache_values[span_index].reshape(slot_count, kv_heads, head_size)
        partials.append(partial_block(query_rows, block_keys, block_values, allowed))
    local_max, local_total, local_sum = tuple(
        (
            jnp.concatenate([block_terms[member] for block_terms in partials], axis=0)
            for member in range(3)
        )
    )
    global_max = lax.pmax(local_max, "kv")
    scaled_total, scaled_sum = rescale(local_max, local_total, local_sum, global_max)
    total_all, sum_all = lax.psum((scaled_total, scaled_sum), "kv")
    own_terms = attend_own(queries, 0, keys_new, values_new, span_len)
    attended = normalize(fold_pair((global_max, total_all, sum_all), own_terms))
    return lax.dynamic_slice_in_dim(attended, row_start, share_rows, 0)


def flip_bits(index, mask):
    result = index
    bit = 1
    while bit <= mask:
        if mask & bit:
            result = result + bit * (1 - 2 * lax.rem(lax.div(index, bit), 2))
        bit *= 2
    return result


def attend_kernel(
    devices, span_count, kv_heads, group_size,
    turn_ref, query_ref, key_ref, value_ref, cache_k, cache_v, live_ref, start_ref, out_ref,
    q_slots, q_other, k_buf, v_buf, new_send, new_recv, live_send, live_recv,
    o_send, o_recv, s_send, s_recv,
    q_ssem, q_rsem, o_ssem, o_rsem, s_ssem, s_rsem, cache_ssem, cache_rsem, local_sem,
    misc_ssem, misc_rsem,
):
    share = query_ref.shape[0]
    slots = cache_k.shape[1]
    half_kv = kv_heads // 2
    half_heads = half_kv * group_size
    half_lanes = half_kv * HD
    span_devices = devices // span_count
    span_len = share * span_devices
    scale2 = HD ** (-0.5) * math.log2(math.e)

    me = lax.axis_index("kv")
    half = lax.rem(me, 2)
    near = lax.div(me, span_devices)

    def target(mask):
        return {"kv": flip_bits(me, mask)}

    def lanes(which, width):
        return pl.ds(pl.multiple_of(which * width, 128), width)

    local_copies = []
    for order in range(span_count):
        span = flip_bits(near, order)
        for which, (src, dst) in enumerate(((cache_k, k_buf), (cache_v, v_buf))):
            copy = pltpu.make_async_copy(
                src.at[span, :, lanes(half, half_lanes)],
                dst.at[order, pl.ds(0, slots)],
                local_sem.at[order, which],
            )
            copy.start()
            local_copies.append(copy)

    barrier = pltpu.get_barrier_semaphore()
    for mask in range(1, devices):
        pl.semaphore_signal(barrier, inc=1, device_id=target(mask), device_id_type=MESH)

    first_token = me * share
    position = (
        start_ref[near]
        + (first_token - near * span_len)
        + lax.broadcasted_iota(jnp.int32, (share, HD), 0)
    )
    angles = (position * turn_ref[...]).astype(jnp.float32) * (2.0 * np.pi / 2.0**32)
    cosine = jnp.cos(angles)
    lane = lax.broadcasted_iota(jnp.int32, (share, HD), 1)
    sine = jnp.sin(angles)
    sine = jnp.where(lane < HD // 2, -sine, sine)

    def rotated(ref, offset):
        x = ref[:, pl.ds(pl.multiple_of(offset, 128), HD)].astype(jnp.float32)
        return x * cosine + pltpu.roll(x, HD // 2, 1) * sine

    for which, dst in ((half, q_slots.at[0]), (1 - half, q_other)):
        for head in range(0, half_heads, 2):
            offset = which * (half_heads * HD) + head * HD
            pair = jnp.concatenate(
                [rotated(query_ref, offset), rotated(query_ref, offset + HD)], axis=0
            )
            dst[head * share : (head + 2) * share, :] = pair.astype(jnp.bfloat16)

    def new_rows(which):
        keys = jnp.concatenate(
            [rotated(key_ref, which * half_lanes + g * HD) for g in range(half_kv)], axis=1
        )
        values = value_ref[:, lanes(which, half_lanes)].astype(jnp.float32)
        return keys, values

    other_keys, other_values = new_rows(1 - half)
    new_send[...] = jnp.concatenate([other_keys, other_values], axis=0).astype(jnp.bfloat16)
    own_keys, own_values = new_rows(half)
    live_row = lax.broadcasted_iota(jnp.int32, live_send.shape, 0)
    live_tile = jnp.zeros(live_send.shape, jnp.int32)
    for order in range(span_count):
        live_tile = jnp.where(live_row == order, live_ref[flip_bits(near, order), 0], live_tile)
    live_send[...] = live_tile

    pl.semaphore_wait(barrier, devices - 1)

    def remote(src, dst, ssem, rsem, mask):
        return pltpu.make_async_remote_copy(
            src_ref=src, dst_ref=dst, send_sem=ssem, recv_sem=rsem,
            device_id=target(mask), device_id_type=MESH,
        )

    q_copies = {}
    for mask in range(1, devices):
        src = q_slots.at[0] if mask % 2 == 0 else q_other
        q_copies[mask] = remote(src, q_slots.at[mask], q_ssem.at[mask], q_rsem.at[mask], mask)
    for mask in range(devices - 1, span_devices - 1, -1):
        q_copies[mask].start()
    for mask in range(1, span_devices):
        q_copies[mask].start()
    cache_copies = {}
    for order in range(span_count):
        span = flip_bits(near, order)
        for which, (src, dst) in enumerate(((cache_k, k_buf), (cache_v, v_buf))):
            copy = remote(
                src.at[span, :, lanes(1 - half, half_lanes)],
                dst.at[order, pl.ds(slots, slots)],
                cache_ssem.at[order, which], cache_rsem.at[order, which], 1,
            )
            copy.start()
            cache_copies[order, which] = copy
        if order == 0:
            new_copy = remote(new_send, new_recv, misc_ssem.at[0], misc_rsem.at[0], 1)
            new_copy.start()
            live_copy = remote(live_send, live_recv, misc_ssem.at[1], misc_rsem.at[1], 1)
            live_copy.start()

    stat_lane = lax.broadcasted_iota(jnp.int32, (share, HD), 1)
    group_rows = group_size * share
    o_copies = []

    for order in range(span_count):
        first_slot = order * span_devices
        for mask in range(max(first_slot, 1), first_slot + span_devices):
            q_copies[mask].wait_recv()
        if order == 0:
            new_copy.wait_recv()
            live_copy.wait_recv()
        local_copies[2 * order].wait()
        local_copies[2 * order + 1].wait()
        cache_copies[order, 0].wait_recv()
        cache_copies[order, 1].wait_recv()

        column = lax.broadcasted_iota(jnp.int32, (1, slots), 1)
        own_live = live_ref[flip_bits(near, order), 0]
        peer_live = jnp.broadcast_to(live_recv[order : order + 1, 0:1], (1, slots))
        bias = jnp.concatenate(
            [
                jnp.where(column < own_live, 0.0, NEG_FILL),
                jnp.where(column < peer_live, 0.0, NEG_FILL),
            ],
            axis=1,
        )
        row_total = span_devices * group_rows
        if order == 0:
            filler = jnp.zeros((HD - 2 * share, half_lanes), jnp.float32)
            received = new_recv[...].astype(jnp.float32)
            new_keys = jnp.concatenate(
                [own_keys, received[:share], filler], axis=0
            ).astype(jnp.bfloat16)
            new_values = jnp.concatenate(
                [own_values, received[share:], filler], axis=0
            ).astype(jnp.bfloat16)
            pieces = []
            key_column = lax.broadcasted_iota(jnp.int32, (share, HD), 1)
            token_row = lax.broadcasted_iota(jnp.int32, (share, HD), 0)
            key_token = jnp.where(
                key_column < share,
                first_token + key_column,
                flip_bits(me, 1) * share + key_column - share,
            )
            for mask in range(span_devices):
                admitted = (key_column < 2 * share) & (
                    key_token <= flip_bits(me, mask) * share + token_row
                )
                piece = jnp.where(admitted, 0.0, NEG_FILL)
                pieces.extend([piece] * group_size)
            new_bias = jnp.concatenate(pieces, axis=0)

        stats = [jnp.zeros((share, HD), jnp.float32) for unused in range(span_devices)]
        for g in range(half_kv):
            queries = q_slots[
                first_slot : first_slot + span_devices, g * group_rows : (g + 1) * group_rows, :
            ].reshape(row_total, HD)
            head_lanes = slice(g * HD, (g + 1) * HD)
            nt = (((1,), (1,)), ((), ()))
            scores = lax.dot_general(
                queries, k_buf[order, :, head_lanes], nt, preferred_element_type=jnp.float32
            ) + bias
            maxima = jnp.max(scores, axis=1, keepdims=True)
            if order == 0:
                new_scores = lax.dot_general(
                    queries, new_keys[:, head_lanes], nt, preferred_element_type=jnp.float32
                ) + new_bias
                maxima = jnp.maximum(maxima, jnp.max(new_scores, axis=1, keepdims=True))
            maxima = jnp.maximum(maxima, NEG_FLOOR)
            weights = jnp.exp2((scores - maxima) * scale2)
            totals = jnp.sum(weights, axis=1, keepdims=True)
            sums = jnp.dot(
                weights.astype(jnp.bfloat16), v_buf[order, :, head_lanes],
                preferred_element_type=jnp.float32,
            )
            if order == 0:
                new_weights = jnp.exp2((new_scores - maxima) * scale2)
                totals = totals + jnp.sum(new_weights, axis=1, keepdims=True)
                sums = sums + jnp.dot(
                    new_weights.astype(jnp.bfloat16), new_values[:, head_lanes],
                    preferred_element_type=jnp.float32,
                )
            o_send[
                first_slot : first_slot + span_devices, g * group_rows : (g + 1) * group_rows, :
            ] = sums.astype(jnp.bfloat16).reshape(span_devices, group_rows, HD)
            for member in range(span_devices):
                for h in range(group_size):
                    begin = member * group_rows + h * share
                    where = g * group_size + h
                    stats[member] = jnp.where(
                        stat_lane == where, maxima[begin : begin + share], stats[member]
                    )
                    stats[member] = jnp.where(
                        stat_lane == where + HD // 2, totals[begin : begin + share], stats[member]
                    )
        for member in range(span_devices):
            s_send[first_slot + member] = stats[member]
        for member in reversed(range(span_devices)):
            mask = first_slot + member
            if mask == 0:
                continue
            for src, dst, ssem, rsem in (
                (s_send, s_recv, s_ssem, s_rsem),
                (o_send, o_recv, o_ssem, o_rsem),
            ):
                copy = remote(src.at[mask], dst.at[mask], ssem.at[mask], rsem.at[mask], mask)
                copy.start()
                o_copies.append(copy)

    for copy in o_copies:
        copy.wait_recv()

    for parity in range(2):
        masks = list(range(parity, devices, 2))
        stat = [s_send[0] if mask == 0 else s_recv[mask] for mask in masks]
        top = functools.reduce(jnp.maximum, stat)
        factors = [jnp.exp2((s - top) * scale2) for s in stat]
        total = functools.reduce(
            jnp.add, [f * pltpu.roll(s, HD // 2, 1) for f, s in zip(factors, stat)]
        )
        inverse = 1.0 / total
        accumulated = [None] * half_heads
        for f, mask in zip(factors, masks):
            weight = f * inverse
            block = (o_send[0] if mask == 0 else o_recv[mask]).astype(jnp.float32)
            for head in range(half_heads):
                term = weight[:, head : head + 1] * block[head * share : (head + 1) * share]
                accumulated[head] = (
                    term if accumulated[head] is None else accumulated[head] + term
                )
        which = half if parity == 0 else 1 - half
        out_ref[:, lanes(which, half_heads * HD)] = jnp.concatenate(
            accumulated, axis=1
        ).astype(jnp.bfloat16)

    for copy in list(q_copies.values()) + list(cache_copies.values()) + o_copies:
        copy.wait_send()
    new_copy.wait_send()
    live_copy.wait_send()


def fused_device(query_in, key_in, value_in, cache_keys, cache_values, live_slots, span_starts):
    devices = lax.axis_size("kv")
    share = query_in.shape[0]
    spans, slots, kv_width = cache_keys.shape
    kv_heads = kv_width // HD
    group_size = query_in.shape[1] // kv_width
    half_kv = kv_heads // 2
    rows = half_kv * group_size * share
    turns = jnp.concatenate([turn_table(HD)] * 2)[None, :]
    vmem = pl.BlockSpec(memory_space=pltpu.VMEM)
    smem = pl.BlockSpec(memory_space=pltpu.SMEM)
    hbm = pl.BlockSpec(memory_space=pl.ANY)
    dma = pltpu.SemaphoreType.DMA
    bf16 = jnp.bfloat16
    return pl.pallas_call(
        functools.partial(attend_kernel, devices, spans, kv_heads, group_size),
        out_shape=jax.ShapeDtypeStruct(query_in.shape, bf16),
        in_specs=[vmem, vmem, vmem, vmem, hbm, hbm, smem, smem],
        out_specs=vmem,
        scratch_shapes=[
            pltpu.VMEM((devices, rows, HD), bf16),
            pltpu.VMEM((rows, HD), bf16),
            pltpu.VMEM((spans, 2 * slots, half_kv * HD), bf16),
            pltpu.VMEM((spans, 2 * slots, half_kv * HD), bf16),
            pltpu.VMEM((2 * share, half_kv * HD), bf16),
            pltpu.VMEM((2 * share, half_kv * HD), bf16),
            pltpu.VMEM((8, HD), jnp.int32),
            pltpu.VMEM((8, HD), jnp.int32),
            pltpu.VMEM((devices, rows, HD), bf16),
            pltpu.VMEM((devices, rows, HD), bf16),
            pltpu.VMEM((devices, share, HD), jnp.float32),
            pltpu.VMEM((devices, share, HD), jnp.float32),
            dma((devices,)), dma((devices,)), dma((devices,)), dma((devices,)),
            dma((devices,)), dma((devices,)),
            dma((spans, 2)), dma((spans, 2)), dma((spans, 2)),
            dma((2,)), dma((2,)),
        ],
        compiler_params=pltpu.CompilerParams(
            collective_id=0, has_side_effects=True, vmem_limit_bytes=40 * 2**20
        ),
        name="fused_attention",
    )(turns, query_in, key_in, value_in, cache_keys, cache_values, live_slots, span_starts)


def is_power(number):
    return number > 0 and number & (number - 1) == 0


def fits_kernel(query_in, key_in, cache_keys, span_starts):
    devices = lax.axis_size("kv")
    spans = span_starts.shape[0]
    kv_heads = key_in.shape[1] // HD
    return (
        is_power(devices)
        and is_power(spans)
        and devices >= 2 * spans
        and query_in.shape[0] == 8
        and kv_heads % 2 == 0
        and query_in.shape[1] % key_in.shape[1] == 0
        and cache_keys.shape[1] % 128 == 0
        and spans <= 8
        and kv_heads // 2 * (query_in.shape[1] // key_in.shape[1]) <= 64
    )


def one_device(query_in, key_in, value_in, cache_keys, cache_values, live_slots, span_starts):
    arrays = (query_in, key_in, value_in, cache_keys, cache_values, live_slots, span_starts)
    if fits_kernel(query_in, key_in, cache_keys, span_starts):
        return fused_device(*arrays)
    return per_device(*arrays)


def solution(mesh):
    in_specs = (
        P(("groups", "kv"), None),
        P(("groups", "kv"), None),
        P(("groups", "kv"), None),
        P("groups", "kv", None),
        P("groups", "kv", None),
        P("groups", "kv"),
        P("groups"),
    )
    out_specs = P(("groups", "kv"), None)
    return jax.shard_map(
        one_device, mesh=mesh, in_specs=in_specs, out_specs=out_specs, check_vma=False
    )
```

```python
import functools
import math

import jax
import jax.numpy as jnp
import numpy as np
from jax import lax
from jax.experimental import pallas as pl
from jax.experimental.pallas import tpu as pltpu
from jax.sharding import PartitionSpec as P

HD = 128


NEG_FILL = -1e30
NEG_FLOOR = -1e29
MESH = pl.DeviceIdType.MESH


def turn_table(head_size):
    half_size = head_size // 2
    frequency = 500000.0 ** (-np.arange(half_size) * 2.0 / head_size)
    turn_counts = np.floor(frequency / (2.0 * np.pi) * 2.0**32 + 0.5).astype(np.int64) % 2**32
    turn_counts = np.where(turn_counts >= 2**31, turn_counts - 2**32, turn_counts)
    return jnp.asarray(turn_counts.astype(np.int32))


def rotate_pairs(values, positions):
    half_size = values.shape[-1] // 2
    phases = positions[:, None] * turn_table(values.shape[-1])[None, :]
    angles = phases.astype(jnp.float32) * (2.0 * np.pi / 2.0**32)
    cosine = jnp.cos(angles)[:, None, :]
    sine_table = jnp.sin(angles)[:, None, :]
    first_half = values[..., :half_size]
    second_half = values[..., half_size:]
    return jnp.concatenate(
        [
            first_half * cosine - second_half * sine_table,
            second_half * cosine + first_half * sine_table,
        ],
        axis=-1,
    )


def partial_block(query_rows, block_keys, block_values, allowed):
    row_count = query_rows.shape[0]
    kv_heads = block_keys.shape[1]
    head_size = block_keys.shape[2]
    grouped = query_rows.reshape(row_count, kv_heads, -1, head_size)
    scores = jnp.einsum(
        "rkgd,skd->kgrs", grouped, block_keys, preferred_element_type=jnp.float32
    ) * head_size ** (-0.5)
    scores = jnp.where(allowed, scores, NEG_FILL)
    maxima = jnp.max(scores, axis=-1)
    weights = jnp.where(allowed, jnp.exp(scores - maxima[..., None]), 0.0)
    totals = jnp.sum(weights, axis=-1)
    weighted_sum = jnp.einsum(
        "kgrs,skd->rkgd",
        weights.astype(jnp.bfloat16),
        block_values,
        preferred_element_type=jnp.float32,
    )
    return (
        jnp.transpose(maxima, (2, 0, 1)).reshape(row_count, -1),
        jnp.transpose(totals, (2, 0, 1)).reshape(row_count, -1),
        weighted_sum.reshape(row_count, -1),
    )


def fold_pair(first_terms, second_terms):
    first_max, first_total, first_sum = first_terms
    second_max, second_total, second_sum = second_terms
    joint_max = jnp.maximum(first_max, second_max)
    first_factor = jnp.exp(first_max - joint_max)
    second_factor = jnp.exp(second_max - joint_max)
    row_count, head_count = joint_max.shape
    weighted = (
        first_sum.reshape(row_count, head_count, -1) * first_factor[..., None]
        + second_sum.reshape(row_count, head_count, -1) * second_factor[..., None]
    )
    return (
        joint_max,
        first_total * first_factor + second_total * second_factor,
        weighted.reshape(row_count, -1),
    )


def rescale(local_max, local_total, local_sum, global_max):
    factor = jnp.exp(local_max - global_max)
    row_count, head_count = factor.shape
    scaled_sum = (local_sum.reshape(row_count, head_count, -1) * factor[..., None]).reshape(
        row_count, -1
    )
    return (local_total * factor, scaled_sum)


def normalize(combined):
    unused_max, totals, sums = combined
    row_count, head_count = totals.shape
    return (
        (sums.reshape(row_count, head_count, -1) / totals[..., None])
        .reshape(row_count, -1)
        .astype(jnp.bfloat16)
    )


def attend_own(query_rows, row_start, keys_new, values_new, span_len):
    query_count = query_rows.shape[0]
    rows_each = min(query_count, span_len)
    blocks = max(query_count // span_len, 1)
    pieces = []
    for block_index in range(blocks):
        first_row = row_start + block_index * rows_each
        key_start = first_row // span_len * span_len
        block_keys = lax.dynamic_slice_in_dim(keys_new, key_start, span_len, 0)
        block_values = lax.dynamic_slice_in_dim(values_new, key_start, span_len, 0)
        allowed = (
            first_row - key_start + jnp.arange(rows_each)[:, None] >= jnp.arange(span_len)[None, :]
        )
        block_rows = query_rows[block_index * rows_each : (block_index + 1) * rows_each]
        pieces.append(partial_block(block_rows, block_keys, block_values, allowed))
    return tuple(
        (
            jnp.concatenate([block_terms[member] for block_terms in pieces], axis=0)
            for member in range(3)
        )
    )


def per_device(query_in, key_in, value_in, cache_keys, cache_values, live_slots, span_starts):
    devices = lax.axis_size("kv")
    device_index = lax.axis_index("kv")
    share_rows = query_in.shape[0]
    token_count = share_rows * devices
    span_count = span_starts.shape[0]
    span_len = token_count // span_count
    head_size = HD
    head_count = query_in.shape[1] // head_size
    kv_heads = key_in.shape[1] // head_size
    row_start = device_index * share_rows
    positions = (span_starts[:, None] + jnp.arange(span_len, dtype=jnp.int32)[None, :]).reshape(
        token_count
    )
    full_query, full_key, full_value = (
        lax.all_gather(query_in, "kv", axis=0, tiled=True),
        lax.all_gather(key_in, "kv", axis=0, tiled=True),
        lax.all_gather(value_in, "kv", axis=0, tiled=True),
    )
    queries = rotate_pairs(
        full_query.astype(jnp.float32).reshape(token_count, head_count, head_size), positions
    ).astype(jnp.bfloat16)
    keys_new = rotate_pairs(
        full_key.astype(jnp.float32).reshape(token_count, kv_heads, head_size), positions
    ).astype(jnp.bfloat16)
    values_new = full_value.reshape(token_count, kv_heads, head_size)
    slot_count = cache_keys.shape[1]
    slot_index = jnp.arange(slot_count)
    partials = []
    for span_index in range(span_count):
        query_rows = queries[span_index * span_len : (span_index + 1) * span_len]
        allowed = (slot_index < live_slots[span_index, 0])[None, :]
        block_keys = cache_keys[span_index].reshape(slot_count, kv_heads, head_size)
        block_values = cache_values[span_index].reshape(slot_count, kv_heads, head_size)
        partials.append(partial_block(query_rows, block_keys, block_values, allowed))
    local_max, local_total, local_sum = tuple(
        (
            jnp.concatenate([block_terms[member] for block_terms in partials], axis=0)
            for member in range(3)
        )
    )
    global_max = lax.pmax(local_max, "kv")
    scaled_total, scaled_sum = rescale(local_max, local_total, local_sum, global_max)
    total_all, sum_all = lax.psum((scaled_total, scaled_sum), "kv")
    own_terms = attend_own(queries, 0, keys_new, values_new, span_len)
    attended = normalize(fold_pair((global_max, total_all, sum_all), own_terms))
    return lax.dynamic_slice_in_dim(attended, row_start, share_rows, 0)


def flip_bits(index, mask):
    result = index
    bit = 1
    while bit <= mask:
        if mask & bit:
            result = result + bit * (1 - 2 * lax.rem(lax.div(index, bit), 2))
        bit *= 2
    return result


def attend_kernel(
    devices, span_count, kv_heads, group_size,
    turn_hbm, query_hbm, key_hbm, value_hbm, cache_k, cache_v, live_hbm, start_hbm, out_ref,
    turn_ref, query_ref, key_ref, value_ref, live_ref, start_ref, in_sem,
    q_slots, q_other, k_buf, v_buf, new_send, new_recv, live_send, live_recv,
    o_send, o_recv, s_send, s_recv,
    q_ssem, q_rsem, o_ssem, o_rsem, s_ssem, s_rsem, cache_ssem, cache_rsem, local_sem,
    misc_ssem, misc_rsem,
):
    share = query_hbm.shape[0]
    slots = cache_k.shape[1]
    half_kv = kv_heads // 2
    half_heads = half_kv * group_size
    half_lanes = half_kv * HD
    span_devices = devices // span_count
    span_len = share * span_devices
    scale2 = HD ** (-0.5) * math.log2(math.e)

    me = lax.axis_index("kv")
    half = lax.rem(me, 2)
    near = lax.div(me, span_devices)

    def target(mask):
        return {"kv": flip_bits(me, mask)}

    def lanes(which, width):
        return pl.ds(pl.multiple_of(which * width, 128), width)

    barrier = pltpu.get_barrier_semaphore()
    for mask in range(1, devices):
        pl.semaphore_signal(barrier, inc=1, device_id=target(mask), device_id_type=MESH)

    operand_copies = []
    for index, (src, dst) in enumerate(
        (
            (start_hbm, start_ref), (turn_hbm, turn_ref), (query_hbm, query_ref),
            (key_hbm, key_ref), (value_hbm, value_ref), (live_hbm, live_ref),
        )
    ):
        copy = pltpu.make_async_copy(src, dst, in_sem.at[index])
        copy.start()
        operand_copies.append(copy)

    local_copies = []
    for order in range(span_count):
        span = flip_bits(near, order)
        for which, (src, dst) in enumerate(((cache_k, k_buf), (cache_v, v_buf))):
            copy = pltpu.make_async_copy(
                src.at[span, :, lanes(half, half_lanes)],
                dst.at[order, pl.ds(0, slots)],
                local_sem.at[order, which],
            )
            copy.start()
            local_copies.append(copy)

    for copy in operand_copies:
        copy.wait()
    first_token = me * share
    position = (
        start_ref[near]
        + (first_token - near * span_len)
        + lax.broadcasted_iota(jnp.int32, (share, HD), 0)
    )
    angles = (position * turn_ref[...]).astype(jnp.float32) * (2.0 * np.pi / 2.0**32)
    cosine = jnp.cos(angles)
    lane = lax.broadcasted_iota(jnp.int32, (share, HD), 1)
    sine = jnp.sin(angles)
    sine = jnp.where(lane < HD // 2, -sine, sine)

    def rotated(ref, offset):
        x = ref[:, pl.ds(pl.multiple_of(offset, 128), HD)].astype(jnp.float32)
        return x * cosine + pltpu.roll(x, HD // 2, 1) * sine

    for which, dst in ((half, q_slots.at[0]), (1 - half, q_other)):
        for head in range(0, half_heads, 2):
            offset = which * (half_heads * HD) + head * HD
            pair = jnp.concatenate(
                [rotated(query_ref, offset), rotated(query_ref, offset + HD)], axis=0
            )
            dst[head * share : (head + 2) * share, :] = pair.astype(jnp.bfloat16)

    def new_rows(which):
        keys = jnp.concatenate(
            [rotated(key_ref, which * half_lanes + g * HD) for g in range(half_kv)], axis=1
        )
        values = value_ref[:, lanes(which, half_lanes)].astype(jnp.float32)
        return keys, values

    other_keys, other_values = new_rows(1 - half)
    new_send[...] = jnp.concatenate([other_keys, other_values], axis=0).astype(jnp.bfloat16)
    own_keys, own_values = new_rows(half)
    live_row = lax.broadcasted_iota(jnp.int32, live_send.shape, 0)
    live_tile = jnp.zeros(live_send.shape, jnp.int32)
    for order in range(span_count):
        live_tile = jnp.where(live_row == order, live_ref[0, flip_bits(near, order)], live_tile)
    live_send[...] = live_tile

    pl.semaphore_wait(barrier, devices - 1)

    def remote(src, dst, ssem, rsem, mask):
        return pltpu.make_async_remote_copy(
            src_ref=src, dst_ref=dst, send_sem=ssem, recv_sem=rsem,
            device_id=target(mask), device_id_type=MESH,
        )

    q_copies = {}
    for mask in range(1, devices):
        src = q_slots.at[0] if mask % 2 == 0 else q_other
        q_copies[mask] = remote(src, q_slots.at[mask], q_ssem.at[mask], q_rsem.at[mask], mask)
    for mask in range(devices - 1, span_devices - 1, -1):
        q_copies[mask].start()
    for mask in range(1, span_devices):
        q_copies[mask].start()
    cache_copies = {}
    for order in range(span_count):
        span = flip_bits(near, order)
        for which, (src, dst) in enumerate(((cache_k, k_buf), (cache_v, v_buf))):
            copy = remote(
                src.at[span, :, lanes(1 - half, half_lanes)],
                dst.at[order, pl.ds(slots, slots)],
                cache_ssem.at[order, which], cache_rsem.at[order, which], 1,
            )
            copy.start()
            cache_copies[order, which] = copy
        if order == 0:
            new_copy = remote(new_send, new_recv, misc_ssem.at[0], misc_rsem.at[0], 1)
            new_copy.start()
            live_copy = remote(live_send, live_recv, misc_ssem.at[1], misc_rsem.at[1], 1)
            live_copy.start()

    stat_lane = lax.broadcasted_iota(jnp.int32, (share, HD), 1)
    group_rows = group_size * share
    o_copies = []

    for order in range(span_count):
        first_slot = order * span_devices
        for mask in range(max(first_slot, 1), first_slot + span_devices):
            q_copies[mask].wait_recv()
        if order == 0:
            new_copy.wait_recv()
            live_copy.wait_recv()
        local_copies[2 * order].wait()
        local_copies[2 * order + 1].wait()
        cache_copies[order, 0].wait_recv()
        cache_copies[order, 1].wait_recv()

        column = lax.broadcasted_iota(jnp.int32, (1, slots), 1)
        own_live = live_ref[0, flip_bits(near, order)]
        peer_live = jnp.broadcast_to(live_recv[order : order + 1, 0:1], (1, slots))
        bias = jnp.concatenate(
            [
                jnp.where(column < own_live, 0.0, NEG_FILL),
                jnp.where(column < peer_live, 0.0, NEG_FILL),
            ],
            axis=1,
        )
        row_total = span_devices * group_rows
        if order == 0:
            filler = jnp.zeros((HD - 2 * share, half_lanes), jnp.float32)
            received = new_recv[...].astype(jnp.float32)
            new_keys = jnp.concatenate(
                [own_keys, received[:share], filler], axis=0
            ).astype(jnp.bfloat16)
            new_values = jnp.concatenate(
                [own_values, received[share:], filler], axis=0
            ).astype(jnp.bfloat16)
            pieces = []
            key_column = lax.broadcasted_iota(jnp.int32, (share, HD), 1)
            token_row = lax.broadcasted_iota(jnp.int32, (share, HD), 0)
            key_token = jnp.where(
                key_column < share,
                first_token + key_column,
                flip_bits(me, 1) * share + key_column - share,
            )
            for mask in range(span_devices):
                admitted = (key_column < 2 * share) & (
                    key_token <= flip_bits(me, mask) * share + token_row
                )
                piece = jnp.where(admitted, 0.0, NEG_FILL)
                pieces.extend([piece] * group_size)
            new_bias = jnp.concatenate(pieces, axis=0)

        stats = [jnp.zeros((share, HD), jnp.float32) for unused in range(span_devices)]
        for g in range(half_kv):
            queries = q_slots[
                first_slot : first_slot + span_devices, g * group_rows : (g + 1) * group_rows, :
            ].reshape(row_total, HD)
            head_lanes = slice(g * HD, (g + 1) * HD)
            nt = (((1,), (1,)), ((), ()))
            scores = lax.dot_general(
                queries, k_buf[order, :, head_lanes], nt, preferred_element_type=jnp.float32
            ) + bias
            maxima = jnp.max(scores, axis=1, keepdims=True)
            if order == 0:
                new_scores = lax.dot_general(
                    queries, new_keys[:, head_lanes], nt, preferred_element_type=jnp.float32
                ) + new_bias
                maxima = jnp.maximum(maxima, jnp.max(new_scores, axis=1, keepdims=True))
            maxima = jnp.maximum(maxima, NEG_FLOOR)
            weights = jnp.exp2((scores - maxima) * scale2)
            totals = jnp.sum(weights, axis=1, keepdims=True)
            sums = jnp.dot(
                weights.astype(jnp.bfloat16), v_buf[order, :, head_lanes],
                preferred_element_type=jnp.float32,
            )
            if order == 0:
                new_weights = jnp.exp2((new_scores - maxima) * scale2)
                totals = totals + jnp.sum(new_weights, axis=1, keepdims=True)
                sums = sums + jnp.dot(
                    new_weights.astype(jnp.bfloat16), new_values[:, head_lanes],
                    preferred_element_type=jnp.float32,
                )
            o_send[
                first_slot : first_slot + span_devices, g * group_rows : (g + 1) * group_rows, :
            ] = sums.astype(jnp.bfloat16).reshape(span_devices, group_rows, HD)
            for member in range(span_devices):
                for h in range(group_size):
                    begin = member * group_rows + h * share
                    where = g * group_size + h
                    stats[member] = jnp.where(
                        stat_lane == where, maxima[begin : begin + share], stats[member]
                    )
                    stats[member] = jnp.where(
                        stat_lane == where + HD // 2, totals[begin : begin + share], stats[member]
                    )
        for member in range(span_devices):
            s_send[first_slot + member] = stats[member]
        for member in reversed(range(span_devices)):
            mask = first_slot + member
            if mask == 0:
                continue
            for src, dst, ssem, rsem in (
                (s_send, s_recv, s_ssem, s_rsem),
                (o_send, o_recv, o_ssem, o_rsem),
            ):
                copy = remote(src.at[mask], dst.at[mask], ssem.at[mask], rsem.at[mask], mask)
                copy.start()
                o_copies.append(copy)

    for copy in o_copies:
        copy.wait_recv()

    for parity in range(2):
        masks = list(range(parity, devices, 2))
        stat = [s_send[0] if mask == 0 else s_recv[mask] for mask in masks]
        top = functools.reduce(jnp.maximum, stat)
        factors = [jnp.exp2((s - top) * scale2) for s in stat]
        total = functools.reduce(
            jnp.add, [f * pltpu.roll(s, HD // 2, 1) for f, s in zip(factors, stat)]
        )
        inverse = 1.0 / total
        accumulated = [None] * half_heads
        for f, mask in zip(factors, masks):
            weight = f * inverse
            block = (o_send[0] if mask == 0 else o_recv[mask]).astype(jnp.float32)
            for head in range(half_heads):
                term = weight[:, head : head + 1] * block[head * share : (head + 1) * share]
                accumulated[head] = (
                    term if accumulated[head] is None else accumulated[head] + term
                )
        which = half if parity == 0 else 1 - half
        out_ref[:, lanes(which, half_heads * HD)] = jnp.concatenate(
            accumulated, axis=1
        ).astype(jnp.bfloat16)

    for copy in list(q_copies.values()) + list(cache_copies.values()) + o_copies:
        copy.wait_send()
    new_copy.wait_send()
    live_copy.wait_send()


def fused_device(query_in, key_in, value_in, cache_keys, cache_values, live_slots, span_starts):
    devices = lax.axis_size("kv")
    share = query_in.shape[0]
    spans, slots, kv_width = cache_keys.shape
    kv_heads = kv_width // HD
    group_size = query_in.shape[1] // kv_width
    half_kv = kv_heads // 2
    rows = half_kv * group_size * share
    turns = jnp.concatenate([turn_table(HD)] * 2)[None, :]
    vmem = pl.BlockSpec(memory_space=pltpu.VMEM)
    hbm = pl.BlockSpec(memory_space=pltpu.HBM)
    dma = pltpu.SemaphoreType.DMA
    bf16 = jnp.bfloat16
    return pl.pallas_call(
        functools.partial(attend_kernel, devices, spans, kv_heads, group_size),
        out_shape=jax.ShapeDtypeStruct(query_in.shape, bf16),
        in_specs=[hbm] * 8,
        out_specs=vmem,
        scratch_shapes=[
            pltpu.VMEM(turns.shape, jnp.int32),
            pltpu.VMEM(query_in.shape, bf16),
            pltpu.VMEM(key_in.shape, bf16),
            pltpu.VMEM(value_in.shape, bf16),
            pltpu.SMEM((1, spans), jnp.int32),
            pltpu.SMEM((spans,), jnp.int32),
            dma((6,)),
            pltpu.VMEM((devices, rows, HD), bf16),
            pltpu.VMEM((rows, HD), bf16),
            pltpu.VMEM((spans, 2 * slots, half_kv * HD), bf16),
            pltpu.VMEM((spans, 2 * slots, half_kv * HD), bf16),
            pltpu.VMEM((2 * share, half_kv * HD), bf16),
            pltpu.VMEM((2 * share, half_kv * HD), bf16),
            pltpu.VMEM((8, HD), jnp.int32),
            pltpu.VMEM((8, HD), jnp.int32),
            pltpu.VMEM((devices, rows, HD), bf16),
            pltpu.VMEM((devices, rows, HD), bf16),
            pltpu.VMEM((devices, share, HD), jnp.float32),
            pltpu.VMEM((devices, share, HD), jnp.float32),
            dma((devices,)), dma((devices,)), dma((devices,)), dma((devices,)),
            dma((devices,)), dma((devices,)),
            dma((spans, 2)), dma((spans, 2)), dma((spans, 2)),
            dma((2,)), dma((2,)),
        ],
        compiler_params=pltpu.CompilerParams(
            collective_id=0, has_side_effects=True, vmem_limit_bytes=64 * 2**20 - 65536
        ),
        name="fused_attention",
    )(turns, query_in, key_in, value_in, cache_keys, cache_values, live_slots.T, span_starts)


def is_power(number):
    return number > 0 and number & (number - 1) == 0


def fits_kernel(query_in, key_in, cache_keys, span_starts):
    devices = lax.axis_size("kv")
    spans = span_starts.shape[0]
    kv_heads = key_in.shape[1] // HD
    return (
        is_power(devices)
        and is_power(spans)
        and devices >= 2 * spans
        and query_in.shape[0] == 8
        and kv_heads % 2 == 0
        and query_in.shape[1] % key_in.shape[1] == 0
        and cache_keys.shape[1] % 128 == 0
        and spans <= 8
        and kv_heads // 2 * (query_in.shape[1] // key_in.shape[1]) <= 64
    )


def one_device(query_in, key_in, value_in, cache_keys, cache_values, live_slots, span_starts):
    arrays = (query_in, key_in, value_in, cache_keys, cache_values, live_slots, span_starts)
    if fits_kernel(query_in, key_in, cache_keys, span_starts):
        return fused_device(*arrays)
    return per_device(*arrays)


def solution(mesh):
    in_specs = (
        P(("groups", "kv"), None),
        P(("groups", "kv"), None),
        P(("groups", "kv"), None),
        P("groups", "kv", None),
        P("groups", "kv", None),
        P("groups", "kv"),
        P("groups"),
    )
    out_specs = P(("groups", "kv"), None)
    return jax.shard_map(
        one_device, mesh=mesh, in_specs=in_specs, out_specs=out_specs, check_vma=False
    )
```

```python
import functools
import math

import jax
import jax.numpy as jnp
import numpy as np
from jax import lax
from jax.experimental import pallas as pl
from jax.experimental.pallas import tpu as pltpu
from jax.sharding import PartitionSpec as P

HD = 128


NEG_FILL = -1e30
NEG_FLOOR = -1e29
MESH = pl.DeviceIdType.MESH


def turn_table(head_size):
    half_size = head_size // 2
    frequency = 500000.0 ** (-np.arange(half_size) * 2.0 / head_size)
    turn_counts = np.floor(frequency / (2.0 * np.pi) * 2.0**32 + 0.5).astype(np.int64) % 2**32
    turn_counts = np.where(turn_counts >= 2**31, turn_counts - 2**32, turn_counts)
    return jnp.asarray(turn_counts.astype(np.int32))


def rotate_pairs(values, positions):
    half_size = values.shape[-1] // 2
    phases = positions[:, None] * turn_table(values.shape[-1])[None, :]
    angles = phases.astype(jnp.float32) * (2.0 * np.pi / 2.0**32)
    cosine = jnp.cos(angles)[:, None, :]
    sine_table = jnp.sin(angles)[:, None, :]
    first_half = values[..., :half_size]
    second_half = values[..., half_size:]
    return jnp.concatenate(
        [
            first_half * cosine - second_half * sine_table,
            second_half * cosine + first_half * sine_table,
        ],
        axis=-1,
    )


def partial_block(query_rows, block_keys, block_values, allowed):
    row_count = query_rows.shape[0]
    kv_heads = block_keys.shape[1]
    head_size = block_keys.shape[2]
    grouped = query_rows.reshape(row_count, kv_heads, -1, head_size)
    scores = jnp.einsum(
        "rkgd,skd->kgrs", grouped, block_keys, preferred_element_type=jnp.float32
    ) * head_size ** (-0.5)
    scores = jnp.where(allowed, scores, NEG_FILL)
    maxima = jnp.max(scores, axis=-1)
    weights = jnp.where(allowed, jnp.exp(scores - maxima[..., None]), 0.0)
    totals = jnp.sum(weights, axis=-1)
    weighted_sum = jnp.einsum(
        "kgrs,skd->rkgd",
        weights.astype(jnp.bfloat16),
        block_values,
        preferred_element_type=jnp.float32,
    )
    return (
        jnp.transpose(maxima, (2, 0, 1)).reshape(row_count, -1),
        jnp.transpose(totals, (2, 0, 1)).reshape(row_count, -1),
        weighted_sum.reshape(row_count, -1),
    )


def fold_pair(first_terms, second_terms):
    first_max, first_total, first_sum = first_terms
    second_max, second_total, second_sum = second_terms
    joint_max = jnp.maximum(first_max, second_max)
    first_factor = jnp.exp(first_max - joint_max)
    second_factor = jnp.exp(second_max - joint_max)
    row_count, head_count = joint_max.shape
    weighted = (
        first_sum.reshape(row_count, head_count, -1) * first_factor[..., None]
        + second_sum.reshape(row_count, head_count, -1) * second_factor[..., None]
    )
    return (
        joint_max,
        first_total * first_factor + second_total * second_factor,
        weighted.reshape(row_count, -1),
    )


def rescale(local_max, local_total, local_sum, global_max):
    factor = jnp.exp(local_max - global_max)
    row_count, head_count = factor.shape
    scaled_sum = (local_sum.reshape(row_count, head_count, -1) * factor[..., None]).reshape(
        row_count, -1
    )
    return (local_total * factor, scaled_sum)


def normalize(combined):
    unused_max, totals, sums = combined
    row_count, head_count = totals.shape
    return (
        (sums.reshape(row_count, head_count, -1) / totals[..., None])
        .reshape(row_count, -1)
        .astype(jnp.bfloat16)
    )


def attend_own(query_rows, row_start, keys_new, values_new, span_len):
    query_count = query_rows.shape[0]
    rows_each = min(query_count, span_len)
    blocks = max(query_count // span_len, 1)
    pieces = []
    for block_index in range(blocks):
        first_row = row_start + block_index * rows_each
        key_start = first_row // span_len * span_len
        block_keys = lax.dynamic_slice_in_dim(keys_new, key_start, span_len, 0)
        block_values = lax.dynamic_slice_in_dim(values_new, key_start, span_len, 0)
        allowed = (
            first_row - key_start + jnp.arange(rows_each)[:, None] >= jnp.arange(span_len)[None, :]
        )
        block_rows = query_rows[block_index * rows_each : (block_index + 1) * rows_each]
        pieces.append(partial_block(block_rows, block_keys, block_values, allowed))
    return tuple(
        (
            jnp.concatenate([block_terms[member] for block_terms in pieces], axis=0)
            for member in range(3)
        )
    )


def per_device(query_in, key_in, value_in, cache_keys, cache_values, live_slots, span_starts):
    devices = lax.axis_size("kv")
    device_index = lax.axis_index("kv")
    share_rows = query_in.shape[0]
    token_count = share_rows * devices
    span_count = span_starts.shape[0]
    span_len = token_count // span_count
    head_size = HD
    head_count = query_in.shape[1] // head_size
    kv_heads = key_in.shape[1] // head_size
    row_start = device_index * share_rows
    positions = (span_starts[:, None] + jnp.arange(span_len, dtype=jnp.int32)[None, :]).reshape(
        token_count
    )
    full_query, full_key, full_value = (
        lax.all_gather(query_in, "kv", axis=0, tiled=True),
        lax.all_gather(key_in, "kv", axis=0, tiled=True),
        lax.all_gather(value_in, "kv", axis=0, tiled=True),
    )
    queries = rotate_pairs(
        full_query.astype(jnp.float32).reshape(token_count, head_count, head_size), positions
    ).astype(jnp.bfloat16)
    keys_new = rotate_pairs(
        full_key.astype(jnp.float32).reshape(token_count, kv_heads, head_size), positions
    ).astype(jnp.bfloat16)
    values_new = full_value.reshape(token_count, kv_heads, head_size)
    slot_count = cache_keys.shape[1]
    slot_index = jnp.arange(slot_count)
    partials = []
    for span_index in range(span_count):
        query_rows = queries[span_index * span_len : (span_index + 1) * span_len]
        allowed = (slot_index < live_slots[span_index, 0])[None, :]
        block_keys = cache_keys[span_index].reshape(slot_count, kv_heads, head_size)
        block_values = cache_values[span_index].reshape(slot_count, kv_heads, head_size)
        partials.append(partial_block(query_rows, block_keys, block_values, allowed))
    local_max, local_total, local_sum = tuple(
        (
            jnp.concatenate([block_terms[member] for block_terms in partials], axis=0)
            for member in range(3)
        )
    )
    global_max = lax.pmax(local_max, "kv")
    scaled_total, scaled_sum = rescale(local_max, local_total, local_sum, global_max)
    total_all, sum_all = lax.psum((scaled_total, scaled_sum), "kv")
    own_terms = attend_own(queries, 0, keys_new, values_new, span_len)
    attended = normalize(fold_pair((global_max, total_all, sum_all), own_terms))
    return lax.dynamic_slice_in_dim(attended, row_start, share_rows, 0)


def flip_bits(index, mask):
    result = index
    bit = 1
    while bit <= mask:
        if mask & bit:
            result = result + bit * (1 - 2 * lax.rem(lax.div(index, bit), 2))
        bit *= 2
    return result


def attend_kernel(
    devices, span_count, kv_heads, group_size,
    turn_hbm, query_hbm, key_hbm, value_hbm, cache_k, cache_v, live_hbm, start_hbm, out_ref,
    turn_ref, query_ref, key_ref, value_ref, live_ref, start_ref, in_sem,
    q_slots, q_other, k_buf, v_buf, new_send, new_recv, live_send, live_recv,
    o_send, o_recv, s_send, s_recv,
    q_ssem, q_rsem, o_ssem, o_rsem, s_ssem, s_rsem, cache_ssem, cache_rsem, local_sem,
    misc_ssem, misc_rsem,
):
    share = query_hbm.shape[0]
    slots = cache_k.shape[1]
    half_kv = kv_heads // 2
    half_heads = half_kv * group_size
    half_lanes = half_kv * HD
    span_devices = devices // span_count
    span_len = share * span_devices
    scale2 = HD ** (-0.5) * math.log2(math.e)

    me = lax.axis_index("kv")
    half = lax.rem(me, 2)
    near = lax.div(me, span_devices)

    def target(mask):
        return {"kv": flip_bits(me, mask)}

    def lanes(which, width):
        return pl.ds(pl.multiple_of(which * width, 128), width)

    barrier = pltpu.get_barrier_semaphore()
    for mask in range(1, devices):
        pl.semaphore_signal(barrier, inc=1, device_id=target(mask), device_id_type=MESH)

    operand_copies = []
    for index, (src, dst) in enumerate(
        (
            (start_hbm, start_ref), (turn_hbm, turn_ref), (query_hbm, query_ref),
            (key_hbm, key_ref), (value_hbm, value_ref), (live_hbm, live_ref),
        )
    ):
        copy = pltpu.make_async_copy(src, dst, in_sem.at[index])
        copy.start()
        operand_copies.append(copy)

    local_copies = []
    for order in range(span_count):
        span = flip_bits(near, order)
        for which, (src, dst) in enumerate(((cache_k, k_buf), (cache_v, v_buf))):
            copy = pltpu.make_async_copy(
                src.at[span, :, lanes(half, half_lanes)],
                dst.at[order, pl.ds(0, slots)],
                local_sem.at[order, which],
            )
            copy.start()
            local_copies.append(copy)

    for copy in operand_copies:
        copy.wait()
    first_token = me * share
    position = (
        start_ref[near]
        + (first_token - near * span_len)
        + lax.broadcasted_iota(jnp.int32, (share, HD), 0)
    )
    angles = (position * turn_ref[...]).astype(jnp.float32) * (2.0 * np.pi / 2.0**32)
    cosine = jnp.cos(angles)
    lane = lax.broadcasted_iota(jnp.int32, (share, HD), 1)
    sine = jnp.sin(angles)
    sine = jnp.where(lane < HD // 2, -sine, sine)

    def rotated(ref, offset):
        x = ref[:, pl.ds(pl.multiple_of(offset, 128), HD)].astype(jnp.float32)
        return x * cosine + pltpu.roll(x, HD // 2, 1) * sine

    for which, dst in ((half, q_slots.at[0]), (1 - half, q_other)):
        for head in range(0, half_heads, 2):
            offset = which * (half_heads * HD) + head * HD
            pair = jnp.concatenate(
                [rotated(query_ref, offset), rotated(query_ref, offset + HD)], axis=0
            )
            dst[head * share : (head + 2) * share, :] = pair.astype(jnp.bfloat16)

    def new_rows(which):
        keys = jnp.concatenate(
            [rotated(key_ref, which * half_lanes + g * HD) for g in range(half_kv)], axis=1
        )
        values = value_ref[:, lanes(which, half_lanes)].astype(jnp.float32)
        return keys, values

    other_keys, other_values = new_rows(1 - half)
    new_send[...] = jnp.concatenate([other_keys, other_values], axis=0).astype(jnp.bfloat16)
    own_keys, own_values = new_rows(half)
    live_row = lax.broadcasted_iota(jnp.int32, live_send.shape, 0)
    live_tile = jnp.zeros(live_send.shape, jnp.int32)
    for order in range(span_count):
        live_tile = jnp.where(live_row == order, live_ref[0, flip_bits(near, order)], live_tile)
    live_send[...] = live_tile

    pl.semaphore_wait(barrier, devices - 1)

    def remote(src, dst, ssem, rsem, mask):
        return pltpu.make_async_remote_copy(
            src_ref=src, dst_ref=dst, send_sem=ssem, recv_sem=rsem,
            device_id=target(mask), device_id_type=MESH,
        )

    q_copies = {}
    for mask in range(1, devices):
        src = q_slots.at[0] if mask % 2 == 0 else q_other
        q_copies[mask] = remote(src, q_slots.at[mask], q_ssem.at[mask], q_rsem.at[mask], mask)
    split = span_devices // 2
    early = [(order, order * span_devices, split) for order in range(1, span_count)]
    late = [(order, begin + split, split) for order, begin, unused in early]
    units = early + [(0, 0, span_devices)] + late

    cache_copies = {}

    def swap_cache(order):
        span = flip_bits(near, order)
        for which, (src, dst) in enumerate(((cache_k, k_buf), (cache_v, v_buf))):
            copy = remote(
                src.at[span, :, lanes(1 - half, half_lanes)],
                dst.at[order, pl.ds(slots, slots)],
                cache_ssem.at[order, which], cache_rsem.at[order, which], 1,
            )
            copy.start()
            cache_copies[order, which] = copy

    for unused, begin, count in early:
        for mask in range(begin, begin + count):
            q_copies[mask].start()
    live_copy = remote(live_send, live_recv, misc_ssem.at[1], misc_rsem.at[1], 1)
    live_copy.start()
    for order in range(1, span_count):
        swap_cache(order)
    for unused, begin, count in late:
        for mask in range(begin, begin + count):
            q_copies[mask].start()
    for mask in range(1, span_devices):
        q_copies[mask].start()
    new_copy = remote(new_send, new_recv, misc_ssem.at[0], misc_rsem.at[0], 1)
    new_copy.start()
    swap_cache(0)

    stat_lane = lax.broadcasted_iota(jnp.int32, (share, HD), 1)
    group_rows = group_size * share
    o_copies = {mask: [] for mask in range(1, devices)}

    live_copy.wait_recv()
    for order, first_slot, count in units:
        for mask in range(max(first_slot, 1), first_slot + count):
            q_copies[mask].wait_recv()
        if order == 0:
            new_copy.wait_recv()
        if first_slot == order * span_devices:
            local_copies[2 * order].wait()
            local_copies[2 * order + 1].wait()
            cache_copies[order, 0].wait_recv()
            cache_copies[order, 1].wait_recv()

        column = lax.broadcasted_iota(jnp.int32, (1, slots), 1)
        own_live = live_ref[0, flip_bits(near, order)]
        peer_live = jnp.broadcast_to(live_recv[order : order + 1, 0:1], (1, slots))
        bias = jnp.concatenate(
            [
                jnp.where(column < own_live, 0.0, NEG_FILL),
                jnp.where(column < peer_live, 0.0, NEG_FILL),
            ],
            axis=1,
        )
        row_total = count * group_rows
        if order == 0:
            filler = jnp.zeros((HD - 2 * share, half_lanes), jnp.float32)
            received = new_recv[...].astype(jnp.float32)
            new_keys = jnp.concatenate(
                [own_keys, received[:share], filler], axis=0
            ).astype(jnp.bfloat16)
            new_values = jnp.concatenate(
                [own_values, received[share:], filler], axis=0
            ).astype(jnp.bfloat16)
            pieces = []
            key_column = lax.broadcasted_iota(jnp.int32, (share, HD), 1)
            token_row = lax.broadcasted_iota(jnp.int32, (share, HD), 0)
            key_token = jnp.where(
                key_column < share,
                first_token + key_column,
                flip_bits(me, 1) * share + key_column - share,
            )
            for mask in range(span_devices):
                admitted = (key_column < 2 * share) & (
                    key_token <= flip_bits(me, mask) * share + token_row
                )
                piece = jnp.where(admitted, 0.0, NEG_FILL)
                pieces.extend([piece] * group_size)
            new_bias = jnp.concatenate(pieces, axis=0)

        stats = [jnp.zeros((share, HD), jnp.float32) for unused in range(count)]
        for g in range(half_kv):
            queries = q_slots[
                first_slot : first_slot + count, g * group_rows : (g + 1) * group_rows, :
            ].reshape(row_total, HD)
            head_lanes = slice(g * HD, (g + 1) * HD)
            nt = (((1,), (1,)), ((), ()))
            scores = lax.dot_general(
                queries, k_buf[order, :, head_lanes], nt, preferred_element_type=jnp.float32
            ) + bias
            maxima = jnp.max(scores, axis=1, keepdims=True)
            if order == 0:
                new_scores = lax.dot_general(
                    queries, new_keys[:, head_lanes], nt, preferred_element_type=jnp.float32
                ) + new_bias
                maxima = jnp.maximum(maxima, jnp.max(new_scores, axis=1, keepdims=True))
            maxima = jnp.maximum(maxima, NEG_FLOOR)
            weights = jnp.exp2((scores - maxima) * scale2)
            totals = jnp.sum(weights, axis=1, keepdims=True)
            sums = jnp.dot(
                weights.astype(jnp.bfloat16), v_buf[order, :, head_lanes],
                preferred_element_type=jnp.float32,
            )
            if order == 0:
                new_weights = jnp.exp2((new_scores - maxima) * scale2)
                totals = totals + jnp.sum(new_weights, axis=1, keepdims=True)
                sums = sums + jnp.dot(
                    new_weights.astype(jnp.bfloat16), new_values[:, head_lanes],
                    preferred_element_type=jnp.float32,
                )
            o_send[
                first_slot : first_slot + count, g * group_rows : (g + 1) * group_rows, :
            ] = sums.astype(jnp.bfloat16).reshape(count, group_rows, HD)
            for member in range(count):
                for h in range(group_size):
                    begin = member * group_rows + h * share
                    where = g * group_size + h
                    stats[member] = jnp.where(
                        stat_lane == where, maxima[begin : begin + share], stats[member]
                    )
                    stats[member] = jnp.where(
                        stat_lane == where + HD // 2, totals[begin : begin + share], stats[member]
                    )
        for member in range(count):
            s_send[first_slot + member] = stats[member]
        for member in range(count):
            mask = first_slot + member
            if mask == 0:
                continue
            for src, dst, ssem, rsem in (
                (s_send, s_recv, s_ssem, s_rsem),
                (o_send, o_recv, o_ssem, o_rsem),
            ):
                copy = remote(src.at[mask], dst.at[mask], ssem.at[mask], rsem.at[mask], mask)
                copy.start()
                o_copies[mask].append(copy)

    late_masks = [m for unused, begin, count in late for m in range(begin, begin + count)]
    early_masks = [m for m in range(devices) if m not in late_masks]
    state = {}
    for masks in (early_masks, late_masks):
        for mask in masks:
            for copy in o_copies.get(mask, []):
                copy.wait_recv()
        for parity in range(2):
            members = [m for m in masks if m % 2 == parity]
            stat = [s_send[0] if m == 0 else s_recv[m] for m in members]
            top = functools.reduce(jnp.maximum, stat)
            total = None
            accumulated = [None] * half_heads
            if parity in state:
                old_top, old_total, old_accumulated = state[parity]
                top = jnp.maximum(top, old_top)
                factor = jnp.exp2((old_top - top) * scale2)
                total = old_total * factor
                accumulated = [
                    factor[:, head : head + 1] * old_accumulated[head]
                    for head in range(half_heads)
                ]
            for member, s in zip(members, stat):
                factor = jnp.exp2((s - top) * scale2)
                part = factor * pltpu.roll(s, HD // 2, 1)
                total = part if total is None else total + part
                block = (o_send[0] if member == 0 else o_recv[member]).astype(jnp.float32)
                for head in range(half_heads):
                    term = factor[:, head : head + 1] * block[head * share : (head + 1) * share]
                    accumulated[head] = (
                        term if accumulated[head] is None else accumulated[head] + term
                    )
            state[parity] = (top, total, accumulated)

    for parity in range(2):
        unused_top, total, accumulated = state[parity]
        inverse = 1.0 / total
        which = half if parity == 0 else 1 - half
        out_ref[:, lanes(which, half_heads * HD)] = jnp.concatenate(
            [accumulated[head] * inverse[:, head : head + 1] for head in range(half_heads)],
            axis=1,
        ).astype(jnp.bfloat16)

    result_copies = [copy for pair in o_copies.values() for copy in pair]
    for copy in list(q_copies.values()) + list(cache_copies.values()) + result_copies:
        copy.wait_send()
    new_copy.wait_send()
    live_copy.wait_send()


def fused_device(query_in, key_in, value_in, cache_keys, cache_values, live_slots, span_starts):
    devices = lax.axis_size("kv")
    share = query_in.shape[0]
    spans, slots, kv_width = cache_keys.shape
    kv_heads = kv_width // HD
    group_size = query_in.shape[1] // kv_width
    half_kv = kv_heads // 2
    rows = half_kv * group_size * share
    turns = jnp.concatenate([turn_table(HD)] * 2)[None, :]
    vmem = pl.BlockSpec(memory_space=pltpu.VMEM)
    hbm = pl.BlockSpec(memory_space=pltpu.HBM)
    dma = pltpu.SemaphoreType.DMA
    bf16 = jnp.bfloat16
    return pl.pallas_call(
        functools.partial(attend_kernel, devices, spans, kv_heads, group_size),
        out_shape=jax.ShapeDtypeStruct(query_in.shape, bf16),
        in_specs=[hbm] * 8,
        out_specs=vmem,
        scratch_shapes=[
            pltpu.VMEM(turns.shape, jnp.int32),
            pltpu.VMEM(query_in.shape, bf16),
            pltpu.VMEM(key_in.shape, bf16),
            pltpu.VMEM(value_in.shape, bf16),
            pltpu.SMEM((1, spans), jnp.int32),
            pltpu.SMEM((spans,), jnp.int32),
            dma((6,)),
            pltpu.VMEM((devices, rows, HD), bf16),
            pltpu.VMEM((rows, HD), bf16),
            pltpu.VMEM((spans, 2 * slots, half_kv * HD), bf16),
            pltpu.VMEM((spans, 2 * slots, half_kv * HD), bf16),
            pltpu.VMEM((2 * share, half_kv * HD), bf16),
            pltpu.VMEM((2 * share, half_kv * HD), bf16),
            pltpu.VMEM((8, HD), jnp.int32),
            pltpu.VMEM((8, HD), jnp.int32),
            pltpu.VMEM((devices, rows, HD), bf16),
            pltpu.VMEM((devices, rows, HD), bf16),
            pltpu.VMEM((devices, share, HD), jnp.float32),
            pltpu.VMEM((devices, share, HD), jnp.float32),
            dma((devices,)), dma((devices,)), dma((devices,)), dma((devices,)),
            dma((devices,)), dma((devices,)),
            dma((spans, 2)), dma((spans, 2)), dma((spans, 2)),
            dma((2,)), dma((2,)),
        ],
        compiler_params=pltpu.CompilerParams(
            collective_id=0, has_side_effects=True, vmem_limit_bytes=64 * 2**20 - 65536
        ),
        name="fused_attention",
    )(turns, query_in, key_in, value_in, cache_keys, cache_values, live_slots.T, span_starts)


def is_power(number):
    return number > 0 and number & (number - 1) == 0


def fits_kernel(query_in, key_in, cache_keys, span_starts):
    devices = lax.axis_size("kv")
    spans = span_starts.shape[0]
    kv_heads = key_in.shape[1] // HD
    return (
        is_power(devices)
        and is_power(spans)
        and devices >= 2 * spans and spans >= 2
        and query_in.shape[0] == 8
        and kv_heads % 2 == 0
        and query_in.shape[1] % key_in.shape[1] == 0
        and cache_keys.shape[1] % 128 == 0
        and spans <= 8
        and kv_heads // 2 * (query_in.shape[1] // key_in.shape[1]) <= 64
    )


def one_device(query_in, key_in, value_in, cache_keys, cache_values, live_slots, span_starts):
    arrays = (query_in, key_in, value_in, cache_keys, cache_values, live_slots, span_starts)
    if fits_kernel(query_in, key_in, cache_keys, span_starts):
        return fused_device(*arrays)
    return per_device(*arrays)


def solution(mesh):
    in_specs = (
        P(("groups", "kv"), None),
        P(("groups", "kv"), None),
        P(("groups", "kv"), None),
        P("groups", "kv", None),
        P("groups", "kv", None),
        P("groups", "kv"),
        P("groups"),
    )
    out_specs = P(("groups", "kv"), None)
    return jax.shard_map(
        one_device, mesh=mesh, in_specs=in_specs, out_specs=out_specs, check_vma=False
    )
```

```python
import functools
import math

import jax
import jax.numpy as jnp
import numpy as np
from jax import lax
from jax.experimental import pallas as pl
from jax.experimental.pallas import tpu as pltpu
from jax.sharding import PartitionSpec as P

HD = 128


NEG_FILL = -1e30
NEG_FLOOR = -1e29
MESH = pl.DeviceIdType.MESH


def turn_table(head_size):
    half_size = head_size // 2
    frequency = 500000.0 ** (-np.arange(half_size) * 2.0 / head_size)
    turn_counts = np.floor(frequency / (2.0 * np.pi) * 2.0**32 + 0.5).astype(np.int64) % 2**32
    turn_counts = np.where(turn_counts >= 2**31, turn_counts - 2**32, turn_counts)
    return jnp.asarray(turn_counts.astype(np.int32))


def rotate_pairs(values, positions):
    half_size = values.shape[-1] // 2
    phases = positions[:, None] * turn_table(values.shape[-1])[None, :]
    angles = phases.astype(jnp.float32) * (2.0 * np.pi / 2.0**32)
    cosine = jnp.cos(angles)[:, None, :]
    sine_table = jnp.sin(angles)[:, None, :]
    first_half = values[..., :half_size]
    second_half = values[..., half_size:]
    return jnp.concatenate(
        [
            first_half * cosine - second_half * sine_table,
            second_half * cosine + first_half * sine_table,
        ],
        axis=-1,
    )


def partial_block(query_rows, block_keys, block_values, allowed):
    row_count = query_rows.shape[0]
    kv_heads = block_keys.shape[1]
    head_size = block_keys.shape[2]
    grouped = query_rows.reshape(row_count, kv_heads, -1, head_size)
    scores = jnp.einsum(
        "rkgd,skd->kgrs", grouped, block_keys, preferred_element_type=jnp.float32
    ) * head_size ** (-0.5)
    scores = jnp.where(allowed, scores, NEG_FILL)
    maxima = jnp.max(scores, axis=-1)
    weights = jnp.where(allowed, jnp.exp(scores - maxima[..., None]), 0.0)
    totals = jnp.sum(weights, axis=-1)
    weighted_sum = jnp.einsum(
        "kgrs,skd->rkgd",
        weights.astype(jnp.bfloat16),
        block_values,
        preferred_element_type=jnp.float32,
    )
    return (
        jnp.transpose(maxima, (2, 0, 1)).reshape(row_count, -1),
        jnp.transpose(totals, (2, 0, 1)).reshape(row_count, -1),
        weighted_sum.reshape(row_count, -1),
    )


def fold_pair(first_terms, second_terms):
    first_max, first_total, first_sum = first_terms
    second_max, second_total, second_sum = second_terms
    joint_max = jnp.maximum(first_max, second_max)
    first_factor = jnp.exp(first_max - joint_max)
    second_factor = jnp.exp(second_max - joint_max)
    row_count, head_count = joint_max.shape
    weighted = (
        first_sum.reshape(row_count, head_count, -1) * first_factor[..., None]
        + second_sum.reshape(row_count, head_count, -1) * second_factor[..., None]
    )
    return (
        joint_max,
        first_total * first_factor + second_total * second_factor,
        weighted.reshape(row_count, -1),
    )


def rescale(local_max, local_total, local_sum, global_max):
    factor = jnp.exp(local_max - global_max)
    row_count, head_count = factor.shape
    scaled_sum = (local_sum.reshape(row_count, head_count, -1) * factor[..., None]).reshape(
        row_count, -1
    )
    return (local_total * factor, scaled_sum)


def normalize(combined):
    unused_max, totals, sums = combined
    row_count, head_count = totals.shape
    return (
        (sums.reshape(row_count, head_count, -1) / totals[..., None])
        .reshape(row_count, -1)
        .astype(jnp.bfloat16)
    )


def attend_own(query_rows, row_start, keys_new, values_new, span_len):
    query_count = query_rows.shape[0]
    rows_each = min(query_count, span_len)
    blocks = max(query_count // span_len, 1)
    pieces = []
    for block_index in range(blocks):
        first_row = row_start + block_index * rows_each
        key_start = first_row // span_len * span_len
        block_keys = lax.dynamic_slice_in_dim(keys_new, key_start, span_len, 0)
        block_values = lax.dynamic_slice_in_dim(values_new, key_start, span_len, 0)
        allowed = (
            first_row - key_start + jnp.arange(rows_each)[:, None] >= jnp.arange(span_len)[None, :]
        )
        block_rows = query_rows[block_index * rows_each : (block_index + 1) * rows_each]
        pieces.append(partial_block(block_rows, block_keys, block_values, allowed))
    return tuple(
        (
            jnp.concatenate([block_terms[member] for block_terms in pieces], axis=0)
            for member in range(3)
        )
    )


def per_device(query_in, key_in, value_in, cache_keys, cache_values, live_slots, span_starts):
    devices = lax.axis_size("kv")
    device_index = lax.axis_index("kv")
    share_rows = query_in.shape[0]
    token_count = share_rows * devices
    span_count = span_starts.shape[0]
    span_len = token_count // span_count
    head_size = HD
    head_count = query_in.shape[1] // head_size
    kv_heads = key_in.shape[1] // head_size
    row_start = device_index * share_rows
    positions = (span_starts[:, None] + jnp.arange(span_len, dtype=jnp.int32)[None, :]).reshape(
        token_count
    )
    full_query, full_key, full_value = (
        lax.all_gather(query_in, "kv", axis=0, tiled=True),
        lax.all_gather(key_in, "kv", axis=0, tiled=True),
        lax.all_gather(value_in, "kv", axis=0, tiled=True),
    )
    queries = rotate_pairs(
        full_query.astype(jnp.float32).reshape(token_count, head_count, head_size), positions
    ).astype(jnp.bfloat16)
    keys_new = rotate_pairs(
        full_key.astype(jnp.float32).reshape(token_count, kv_heads, head_size), positions
    ).astype(jnp.bfloat16)
    values_new = full_value.reshape(token_count, kv_heads, head_size)
    slot_count = cache_keys.shape[1]
    slot_index = jnp.arange(slot_count)
    partials = []
    for span_index in range(span_count):
        query_rows = queries[span_index * span_len : (span_index + 1) * span_len]
        allowed = (slot_index < live_slots[span_index, 0])[None, :]
        block_keys = cache_keys[span_index].reshape(slot_count, kv_heads, head_size)
        block_values = cache_values[span_index].reshape(slot_count, kv_heads, head_size)
        partials.append(partial_block(query_rows, block_keys, block_values, allowed))
    local_max, local_total, local_sum = tuple(
        (
            jnp.concatenate([block_terms[member] for block_terms in partials], axis=0)
            for member in range(3)
        )
    )
    global_max = lax.pmax(local_max, "kv")
    scaled_total, scaled_sum = rescale(local_max, local_total, local_sum, global_max)
    total_all, sum_all = lax.psum((scaled_total, scaled_sum), "kv")
    own_terms = attend_own(queries, 0, keys_new, values_new, span_len)
    attended = normalize(fold_pair((global_max, total_all, sum_all), own_terms))
    return lax.dynamic_slice_in_dim(attended, row_start, share_rows, 0)


RELAY = 2


def flip_bits(index, mask):
    result = index
    bit = 1
    while bit <= mask:
        if mask & bit:
            result = result + bit * (1 - 2 * lax.rem(lax.div(index, bit), 2))
        bit *= 2
    return result


def attend_kernel(
    devices, span_count, kv_heads, group_size,
    turn_hbm, query_hbm, key_hbm, value_hbm, cache_k, cache_v, live_hbm, start_hbm, out_ref,
    turn_ref, query_ref, key_ref, value_ref, live_ref, start_ref, in_sem,
    q_slots, q_other, k_buf, v_buf, new_send, new_recv, live_send, live_recv,
    o_send, o_recv, s_send, s_recv,
    q_ssem, q_rsem, o_ssem, o_rsem, s_ssem, s_rsem, cache_ssem, cache_rsem, local_sem,
    misc_ssem, misc_rsem,
):
    share = query_hbm.shape[0]
    slots = cache_k.shape[1]
    half_kv = kv_heads // 2
    half_heads = half_kv * group_size
    half_lanes = half_kv * HD
    span_devices = devices // span_count
    span_len = share * span_devices
    scale2 = HD ** (-0.5) * math.log2(math.e)

    me = lax.axis_index("kv")
    half = lax.rem(me, 2)
    near = lax.div(me, span_devices)

    def target(mask):
        return {"kv": flip_bits(me, mask)}

    def lanes(which, width):
        return pl.ds(pl.multiple_of(which * width, 128), width)

    barrier = pltpu.get_barrier_semaphore()
    for mask in range(1, devices):
        pl.semaphore_signal(barrier, inc=1, device_id=target(mask), device_id_type=MESH)

    operand_copies = []
    for index, (src, dst) in enumerate(
        (
            (start_hbm, start_ref), (turn_hbm, turn_ref), (query_hbm, query_ref),
            (key_hbm, key_ref), (value_hbm, value_ref), (live_hbm, live_ref),
        )
    ):
        copy = pltpu.make_async_copy(src, dst, in_sem.at[index])
        copy.start()
        operand_copies.append(copy)

    local_copies = []
    for order in range(span_count):
        span = flip_bits(near, order)
        for which, (src, dst) in enumerate(((cache_k, k_buf), (cache_v, v_buf))):
            copy = pltpu.make_async_copy(
                src.at[span, :, lanes(half, half_lanes)],
                dst.at[order, pl.ds(0, slots)],
                local_sem.at[order, which],
            )
            copy.start()
            local_copies.append(copy)

    for copy in operand_copies:
        copy.wait()
    first_token = me * share
    position = (
        start_ref[near]
        + (first_token - near * span_len)
        + lax.broadcasted_iota(jnp.int32, (share, HD), 0)
    )
    angles = (position * turn_ref[...]).astype(jnp.float32) * (2.0 * np.pi / 2.0**32)
    cosine = jnp.cos(angles)
    lane = lax.broadcasted_iota(jnp.int32, (share, HD), 1)
    sine = jnp.sin(angles)
    sine = jnp.where(lane < HD // 2, -sine, sine)

    def rotated(ref, offset):
        x = ref[:, pl.ds(pl.multiple_of(offset, 128), HD)].astype(jnp.float32)
        return x * cosine + pltpu.roll(x, HD // 2, 1) * sine

    for which, dst in ((half, q_slots.at[0]), (1 - half, q_other)):
        for head in range(0, half_heads, 2):
            offset = which * (half_heads * HD) + head * HD
            pair = jnp.concatenate(
                [rotated(query_ref, offset), rotated(query_ref, offset + HD)], axis=0
            )
            dst[head * share : (head + 2) * share, :] = pair.astype(jnp.bfloat16)

    def new_rows(which):
        keys = jnp.concatenate(
            [rotated(key_ref, which * half_lanes + g * HD) for g in range(half_kv)], axis=1
        )
        values = value_ref[:, lanes(which, half_lanes)].astype(jnp.float32)
        return keys, values

    other_keys, other_values = new_rows(1 - half)
    new_send[...] = jnp.concatenate([other_keys, other_values], axis=0).astype(jnp.bfloat16)
    own_keys, own_values = new_rows(half)
    live_row = lax.broadcasted_iota(jnp.int32, live_send.shape, 0)
    live_tile = jnp.zeros(live_send.shape, jnp.int32)
    for order in range(span_count):
        live_tile = jnp.where(live_row == order, live_ref[0, flip_bits(near, order)], live_tile)
    live_send[...] = live_tile

    pl.semaphore_wait(barrier, devices - 1)

    def remote(src, dst, ssem, rsem, mask):
        return pltpu.make_async_remote_copy(
            src_ref=src, dst_ref=dst, send_sem=ssem, recv_sem=rsem,
            device_id=target(mask), device_id_type=MESH,
        )

    q_copies = {}
    for mask in range(1, devices):
        sems = (q_ssem.at[mask], q_rsem.at[mask])
        if mask & RELAY:
            q_copies[mask] = remote(q_slots.at[mask - RELAY], q_slots.at[mask], *sems, RELAY)
        else:
            src = q_slots.at[0] if mask % 2 == 0 else q_other
            q_copies[mask] = remote(src, q_slots.at[mask], *sems, mask)
    split = span_devices // 2
    early = [(order, order * span_devices, split) for order in range(1, span_count)]
    late = [(order, begin + split, split) for order, begin, unused in early]
    units = early + [(0, 0, span_devices)] + late

    def direct(begin, count):
        return [mask for mask in range(begin, begin + count) if not mask & RELAY]

    cache_copies = {}

    def swap_cache(order):
        span = flip_bits(near, order)
        for which, (src, dst) in enumerate(((cache_k, k_buf), (cache_v, v_buf))):
            copy = remote(
                src.at[span, :, lanes(1 - half, half_lanes)],
                dst.at[order, pl.ds(slots, slots)],
                cache_ssem.at[order, which], cache_rsem.at[order, which], 1,
            )
            copy.start()
            cache_copies[order, which] = copy

    for unused, begin, count in early:
        for mask in direct(begin, count):
            q_copies[mask].start()
    live_copy = remote(live_send, live_recv, misc_ssem.at[1], misc_rsem.at[1], 1)
    live_copy.start()
    for order in range(1, span_count):
        swap_cache(order)
    for unused, begin, count in late:
        for mask in direct(begin, count):
            q_copies[mask].start()
    for mask in direct(1, span_devices - 1):
        q_copies[mask].start()
    q_copies[RELAY].start()
    new_copy = remote(new_send, new_recv, misc_ssem.at[0], misc_rsem.at[0], 1)
    new_copy.start()
    swap_cache(0)

    stat_lane = lax.broadcasted_iota(jnp.int32, (share, HD), 1)
    group_rows = group_size * share
    o_copies = {mask: [] for mask in range(1, devices)}

    for unused, begin, count in early + late + [(0, 1, span_devices - 1)]:
        for mask in direct(begin, count):
            q_copies[mask].wait_recv()
            q_copies[mask + RELAY].start()

    live_copy.wait_recv()
    for order, first_slot, count in units:
        for mask in range(first_slot, first_slot + count):
            if mask & RELAY:
                q_copies[mask].wait_recv()
        if order == 0:
            new_copy.wait_recv()
        if first_slot == order * span_devices:
            local_copies[2 * order].wait()
            local_copies[2 * order + 1].wait()
            cache_copies[order, 0].wait_recv()
            cache_copies[order, 1].wait_recv()

        column = lax.broadcasted_iota(jnp.int32, (1, slots), 1)
        own_live = live_ref[0, flip_bits(near, order)]
        peer_live = jnp.broadcast_to(live_recv[order : order + 1, 0:1], (1, slots))
        bias = jnp.concatenate(
            [
                jnp.where(column < own_live, 0.0, NEG_FILL),
                jnp.where(column < peer_live, 0.0, NEG_FILL),
            ],
            axis=1,
        )
        row_total = count * group_rows
        if order == 0:
            filler = jnp.zeros((HD - 2 * share, half_lanes), jnp.float32)
            received = new_recv[...].astype(jnp.float32)
            new_keys = jnp.concatenate(
                [own_keys, received[:share], filler], axis=0
            ).astype(jnp.bfloat16)
            new_values = jnp.concatenate(
                [own_values, received[share:], filler], axis=0
            ).astype(jnp.bfloat16)
            pieces = []
            key_column = lax.broadcasted_iota(jnp.int32, (share, HD), 1)
            token_row = lax.broadcasted_iota(jnp.int32, (share, HD), 0)
            key_token = jnp.where(
                key_column < share,
                first_token + key_column,
                flip_bits(me, 1) * share + key_column - share,
            )
            for mask in range(span_devices):
                admitted = (key_column < 2 * share) & (
                    key_token <= flip_bits(me, mask) * share + token_row
                )
                piece = jnp.where(admitted, 0.0, NEG_FILL)
                pieces.extend([piece] * group_size)
            new_bias = jnp.concatenate(pieces, axis=0)

        stats = [jnp.zeros((share, HD), jnp.float32) for unused in range(count)]
        for g in range(half_kv):
            queries = q_slots[
                first_slot : first_slot + count, g * group_rows : (g + 1) * group_rows, :
            ].reshape(row_total, HD)
            head_lanes = slice(g * HD, (g + 1) * HD)
            nt = (((1,), (1,)), ((), ()))
            scores = lax.dot_general(
                queries, k_buf[order, :, head_lanes], nt, preferred_element_type=jnp.float32
            ) + bias
            maxima = jnp.max(scores, axis=1, keepdims=True)
            if order == 0:
                new_scores = lax.dot_general(
                    queries, new_keys[:, head_lanes], nt, preferred_element_type=jnp.float32
                ) + new_bias
                maxima = jnp.maximum(maxima, jnp.max(new_scores, axis=1, keepdims=True))
            maxima = jnp.maximum(maxima, NEG_FLOOR)
            weights = jnp.exp2((scores - maxima) * scale2)
            totals = jnp.sum(weights, axis=1, keepdims=True)
            sums = jnp.dot(
                weights.astype(jnp.bfloat16), v_buf[order, :, head_lanes],
                preferred_element_type=jnp.float32,
            )
            if order == 0:
                new_weights = jnp.exp2((new_scores - maxima) * scale2)
                totals = totals + jnp.sum(new_weights, axis=1, keepdims=True)
                sums = sums + jnp.dot(
                    new_weights.astype(jnp.bfloat16), new_values[:, head_lanes],
                    preferred_element_type=jnp.float32,
                )
            o_send[
                first_slot : first_slot + count, g * group_rows : (g + 1) * group_rows, :
            ] = sums.astype(jnp.bfloat16).reshape(count, group_rows, HD)
            for member in range(count):
                for h in range(group_size):
                    begin = member * group_rows + h * share
                    where = g * group_size + h
                    stats[member] = jnp.where(
                        stat_lane == where, maxima[begin : begin + share], stats[member]
                    )
                    stats[member] = jnp.where(
                        stat_lane == where + HD // 2, totals[begin : begin + share], stats[member]
                    )
        for member in range(count):
            s_send[first_slot + member] = stats[member]
        for member in range(count):
            mask = first_slot + member
            if mask == 0:
                continue
            for src, dst, ssem, rsem in (
                (s_send, s_recv, s_ssem, s_rsem),
                (o_send, o_recv, o_ssem, o_rsem),
            ):
                copy = remote(src.at[mask], dst.at[mask], ssem.at[mask], rsem.at[mask], mask)
                copy.start()
                o_copies[mask].append(copy)

    late_masks = [m for unused, begin, count in late for m in range(begin, begin + count)]
    early_masks = [m for m in range(devices) if m not in late_masks]
    state = {}
    for masks in (early_masks, late_masks):
        for mask in masks:
            for copy in o_copies.get(mask, []):
                copy.wait_recv()
        for parity in range(2):
            members = [m for m in masks if m % 2 == parity]
            stat = [s_send[0] if m == 0 else s_recv[m] for m in members]
            top = functools.reduce(jnp.maximum, stat)
            total = None
            accumulated = [None] * half_heads
            if parity in state:
                old_top, old_total, old_accumulated = state[parity]
                top = jnp.maximum(top, old_top)
                factor = jnp.exp2((old_top - top) * scale2)
                total = old_total * factor
                accumulated = [
                    factor[:, head : head + 1] * old_accumulated[head]
                    for head in range(half_heads)
                ]
            for member, s in zip(members, stat):
                factor = jnp.exp2((s - top) * scale2)
                part = factor * pltpu.roll(s, HD // 2, 1)
                total = part if total is None else total + part
                block = (o_send[0] if member == 0 else o_recv[member]).astype(jnp.float32)
                for head in range(half_heads):
                    term = factor[:, head : head + 1] * block[head * share : (head + 1) * share]
                    accumulated[head] = (
                        term if accumulated[head] is None else accumulated[head] + term
                    )
            state[parity] = (top, total, accumulated)

    for parity in range(2):
        unused_top, total, accumulated = state[parity]
        inverse = 1.0 / total
        which = half if parity == 0 else 1 - half
        out_ref[:, lanes(which, half_heads * HD)] = jnp.concatenate(
            [accumulated[head] * inverse[:, head : head + 1] for head in range(half_heads)],
            axis=1,
        ).astype(jnp.bfloat16)

    result_copies = [copy for pair in o_copies.values() for copy in pair]
    for copy in list(q_copies.values()) + list(cache_copies.values()) + result_copies:
        copy.wait_send()
    new_copy.wait_send()
    live_copy.wait_send()


def fused_device(query_in, key_in, value_in, cache_keys, cache_values, live_slots, span_starts):
    devices = lax.axis_size("kv")
    share = query_in.shape[0]
    spans, slots, kv_width = cache_keys.shape
    kv_heads = kv_width // HD
    group_size = query_in.shape[1] // kv_width
    half_kv = kv_heads // 2
    rows = half_kv * group_size * share
    turns = jnp.concatenate([turn_table(HD)] * 2)[None, :]
    vmem = pl.BlockSpec(memory_space=pltpu.VMEM)
    hbm = pl.BlockSpec(memory_space=pltpu.HBM)
    dma = pltpu.SemaphoreType.DMA
    bf16 = jnp.bfloat16
    return pl.pallas_call(
        functools.partial(attend_kernel, devices, spans, kv_heads, group_size),
        out_shape=jax.ShapeDtypeStruct(query_in.shape, bf16),
        in_specs=[hbm] * 8,
        out_specs=vmem,
        scratch_shapes=[
            pltpu.VMEM(turns.shape, jnp.int32),
            pltpu.VMEM(query_in.shape, bf16),
            pltpu.VMEM(key_in.shape, bf16),
            pltpu.VMEM(value_in.shape, bf16),
            pltpu.SMEM((1, spans), jnp.int32),
            pltpu.SMEM((spans,), jnp.int32),
            dma((6,)),
            pltpu.VMEM((devices, rows, HD), bf16),
            pltpu.VMEM((rows, HD), bf16),
            pltpu.VMEM((spans, 2 * slots, half_kv * HD), bf16),
            pltpu.VMEM((spans, 2 * slots, half_kv * HD), bf16),
            pltpu.VMEM((2 * share, half_kv * HD), bf16),
            pltpu.VMEM((2 * share, half_kv * HD), bf16),
            pltpu.VMEM((8, HD), jnp.int32),
            pltpu.VMEM((8, HD), jnp.int32),
            pltpu.VMEM((devices, rows, HD), bf16),
            pltpu.VMEM((devices, rows, HD), bf16),
            pltpu.VMEM((devices, share, HD), jnp.float32),
            pltpu.VMEM((devices, share, HD), jnp.float32),
            dma((devices,)), dma((devices,)), dma((devices,)), dma((devices,)),
            dma((devices,)), dma((devices,)),
            dma((spans, 2)), dma((spans, 2)), dma((spans, 2)),
            dma((2,)), dma((2,)),
        ],
        compiler_params=pltpu.CompilerParams(
            collective_id=0, has_side_effects=True, vmem_limit_bytes=64 * 2**20 - 65536
        ),
        name="fused_attention",
    )(turns, query_in, key_in, value_in, cache_keys, cache_values, live_slots.T, span_starts)


def is_power(number):
    return number > 0 and number & (number - 1) == 0


def fits_kernel(query_in, key_in, cache_keys, span_starts):
    devices = lax.axis_size("kv")
    spans = span_starts.shape[0]
    kv_heads = key_in.shape[1] // HD
    return (
        is_power(devices)
        and is_power(spans)
        and devices >= 8 * spans and spans >= 2
        and query_in.shape[0] == 8
        and kv_heads % 2 == 0
        and query_in.shape[1] % key_in.shape[1] == 0
        and cache_keys.shape[1] % 128 == 0
        and spans <= 8
        and kv_heads // 2 * (query_in.shape[1] // key_in.shape[1]) <= 64
    )


def one_device(query_in, key_in, value_in, cache_keys, cache_values, live_slots, span_starts):
    arrays = (query_in, key_in, value_in, cache_keys, cache_values, live_slots, span_starts)
    if fits_kernel(query_in, key_in, cache_keys, span_starts):
        return fused_device(*arrays)
    return per_device(*arrays)


def solution(mesh):
    in_specs = (
        P(("groups", "kv"), None),
        P(("groups", "kv"), None),
        P(("groups", "kv"), None),
        P("groups", "kv", None),
        P("groups", "kv", None),
        P("groups", "kv"),
        P("groups"),
    )
    out_specs = P(("groups", "kv"), None)
    return jax.shard_map(
        one_device, mesh=mesh, in_specs=in_specs, out_specs=out_specs, check_vma=False
    )
```

```python
import functools
import math

import jax
import jax.numpy as jnp
import numpy as np
from jax import lax
from jax.experimental import pallas as pl
from jax.experimental.pallas import tpu as pltpu
from jax.sharding import PartitionSpec as P

HD = 128


NEG_FILL = -1e30
NEG_FLOOR = -1e29
MESH = pl.DeviceIdType.MESH


def turn_table(head_size):
    half_size = head_size // 2
    frequency = 500000.0 ** (-np.arange(half_size) * 2.0 / head_size)
    turn_counts = np.floor(frequency / (2.0 * np.pi) * 2.0**32 + 0.5).astype(np.int64) % 2**32
    turn_counts = np.where(turn_counts >= 2**31, turn_counts - 2**32, turn_counts)
    return jnp.asarray(turn_counts.astype(np.int32))


def rotate_pairs(values, positions):
    half_size = values.shape[-1] // 2
    phases = positions[:, None] * turn_table(values.shape[-1])[None, :]
    angles = phases.astype(jnp.float32) * (2.0 * np.pi / 2.0**32)
    cosine = jnp.cos(angles)[:, None, :]
    sine_table = jnp.sin(angles)[:, None, :]
    first_half = values[..., :half_size]
    second_half = values[..., half_size:]
    return jnp.concatenate(
        [
            first_half * cosine - second_half * sine_table,
            second_half * cosine + first_half * sine_table,
        ],
        axis=-1,
    )


def partial_block(query_rows, block_keys, block_values, allowed):
    row_count = query_rows.shape[0]
    kv_heads = block_keys.shape[1]
    head_size = block_keys.shape[2]
    grouped = query_rows.reshape(row_count, kv_heads, -1, head_size)
    scores = jnp.einsum(
        "rkgd,skd->kgrs", grouped, block_keys, preferred_element_type=jnp.float32
    ) * head_size ** (-0.5)
    scores = jnp.where(allowed, scores, NEG_FILL)
    maxima = jnp.max(scores, axis=-1)
    weights = jnp.where(allowed, jnp.exp(scores - maxima[..., None]), 0.0)
    totals = jnp.sum(weights, axis=-1)
    weighted_sum = jnp.einsum(
        "kgrs,skd->rkgd",
        weights.astype(jnp.bfloat16),
        block_values,
        preferred_element_type=jnp.float32,
    )
    return (
        jnp.transpose(maxima, (2, 0, 1)).reshape(row_count, -1),
        jnp.transpose(totals, (2, 0, 1)).reshape(row_count, -1),
        weighted_sum.reshape(row_count, -1),
    )


def fold_pair(first_terms, second_terms):
    first_max, first_total, first_sum = first_terms
    second_max, second_total, second_sum = second_terms
    joint_max = jnp.maximum(first_max, second_max)
    first_factor = jnp.exp(first_max - joint_max)
    second_factor = jnp.exp(second_max - joint_max)
    row_count, head_count = joint_max.shape
    weighted = (
        first_sum.reshape(row_count, head_count, -1) * first_factor[..., None]
        + second_sum.reshape(row_count, head_count, -1) * second_factor[..., None]
    )
    return (
        joint_max,
        first_total * first_factor + second_total * second_factor,
        weighted.reshape(row_count, -1),
    )


def rescale(local_max, local_total, local_sum, global_max):
    factor = jnp.exp(local_max - global_max)
    row_count, head_count = factor.shape
    scaled_sum = (local_sum.reshape(row_count, head_count, -1) * factor[..., None]).reshape(
        row_count, -1
    )
    return (local_total * factor, scaled_sum)


def normalize(combined):
    unused_max, totals, sums = combined
    row_count, head_count = totals.shape
    return (
        (sums.reshape(row_count, head_count, -1) / totals[..., None])
        .reshape(row_count, -1)
        .astype(jnp.bfloat16)
    )


def attend_own(query_rows, row_start, keys_new, values_new, span_len):
    query_count = query_rows.shape[0]
    rows_each = min(query_count, span_len)
    blocks = max(query_count // span_len, 1)
    pieces = []
    for block_index in range(blocks):
        first_row = row_start + block_index * rows_each
        key_start = first_row // span_len * span_len
        block_keys = lax.dynamic_slice_in_dim(keys_new, key_start, span_len, 0)
        block_values = lax.dynamic_slice_in_dim(values_new, key_start, span_len, 0)
        allowed = (
            first_row - key_start + jnp.arange(rows_each)[:, None] >= jnp.arange(span_len)[None, :]
        )
        block_rows = query_rows[block_index * rows_each : (block_index + 1) * rows_each]
        pieces.append(partial_block(block_rows, block_keys, block_values, allowed))
    return tuple(
        (
            jnp.concatenate([block_terms[member] for block_terms in pieces], axis=0)
            for member in range(3)
        )
    )


def per_device(query_in, key_in, value_in, cache_keys, cache_values, live_slots, span_starts):
    devices = lax.axis_size("kv")
    device_index = lax.axis_index("kv")
    share_rows = query_in.shape[0]
    token_count = share_rows * devices
    span_count = span_starts.shape[0]
    span_len = token_count // span_count
    head_size = HD
    head_count = query_in.shape[1] // head_size
    kv_heads = key_in.shape[1] // head_size
    row_start = device_index * share_rows
    positions = (span_starts[:, None] + jnp.arange(span_len, dtype=jnp.int32)[None, :]).reshape(
        token_count
    )
    full_query, full_key, full_value = (
        lax.all_gather(query_in, "kv", axis=0, tiled=True),
        lax.all_gather(key_in, "kv", axis=0, tiled=True),
        lax.all_gather(value_in, "kv", axis=0, tiled=True),
    )
    queries = rotate_pairs(
        full_query.astype(jnp.float32).reshape(token_count, head_count, head_size), positions
    ).astype(jnp.bfloat16)
    keys_new = rotate_pairs(
        full_key.astype(jnp.float32).reshape(token_count, kv_heads, head_size), positions
    ).astype(jnp.bfloat16)
    values_new = full_value.reshape(token_count, kv_heads, head_size)
    slot_count = cache_keys.shape[1]
    slot_index = jnp.arange(slot_count)
    partials = []
    for span_index in range(span_count):
        query_rows = queries[span_index * span_len : (span_index + 1) * span_len]
        allowed = (slot_index < live_slots[span_index, 0])[None, :]
        block_keys = cache_keys[span_index].reshape(slot_count, kv_heads, head_size)
        block_values = cache_values[span_index].reshape(slot_count, kv_heads, head_size)
        partials.append(partial_block(query_rows, block_keys, block_values, allowed))
    local_max, local_total, local_sum = tuple(
        (
            jnp.concatenate([block_terms[member] for block_terms in partials], axis=0)
            for member in range(3)
        )
    )
    global_max = lax.pmax(local_max, "kv")
    scaled_total, scaled_sum = rescale(local_max, local_total, local_sum, global_max)
    total_all, sum_all = lax.psum((scaled_total, scaled_sum), "kv")
    own_terms = attend_own(queries, 0, keys_new, values_new, span_len)
    attended = normalize(fold_pair((global_max, total_all, sum_all), own_terms))
    return lax.dynamic_slice_in_dim(attended, row_start, share_rows, 0)


RELAY = 2


def flip_bits(index, mask):
    result = index
    bit = 1
    while bit <= mask:
        if mask & bit:
            result = result + bit * (1 - 2 * lax.rem(lax.div(index, bit), 2))
        bit *= 2
    return result


def attend_kernel(
    devices, span_count, kv_heads, group_size,
    turn_hbm, query_hbm, key_hbm, value_hbm, cache_k, cache_v, live_hbm, start_hbm, out_ref,
    turn_ref, query_ref, key_ref, value_ref, live_ref, start_ref, in_sem,
    q_slots, q_other, k_buf, v_buf, new_send, new_recv, live_send, live_recv,
    o_send, o_recv, s_send, s_recv,
    q_ssem, q_rsem, o_ssem, o_rsem, s_ssem, s_rsem, cache_ssem, cache_rsem, local_sem,
    misc_ssem, misc_rsem,
):
    share = query_hbm.shape[0]
    slots = cache_k.shape[1]
    half_kv = kv_heads // 2
    half_heads = half_kv * group_size
    half_lanes = half_kv * HD
    span_devices = devices // span_count
    span_len = share * span_devices
    scale2 = HD ** (-0.5) * math.log2(math.e)

    me = lax.axis_index("kv")
    half = lax.rem(me, 2)
    near = lax.div(me, span_devices)

    def target(mask):
        return {"kv": flip_bits(me, mask)}

    def lanes(which, width):
        return pl.ds(pl.multiple_of(which * width, 128), width)

    barrier = pltpu.get_barrier_semaphore()
    for mask in range(1, devices):
        pl.semaphore_signal(barrier, inc=1, device_id=target(mask), device_id_type=MESH)

    operand_copies = []
    for index, (src, dst) in enumerate(
        (
            (start_hbm, start_ref), (turn_hbm, turn_ref), (query_hbm, query_ref),
            (key_hbm, key_ref), (value_hbm, value_ref), (live_hbm, live_ref),
        )
    ):
        copy = pltpu.make_async_copy(src, dst, in_sem.at[index])
        copy.start()
        operand_copies.append(copy)

    local_copies = []
    for order in range(span_count):
        span = flip_bits(near, order)
        for which, (src, dst) in enumerate(((cache_k, k_buf), (cache_v, v_buf))):
            copy = pltpu.make_async_copy(
                src.at[span, :, lanes(half, half_lanes)],
                dst.at[order, pl.ds(0, slots)],
                local_sem.at[order, which],
            )
            copy.start()
            local_copies.append(copy)

    for copy in operand_copies:
        copy.wait()
    first_token = me * share
    position = (
        start_ref[near]
        + (first_token - near * span_len)
        + lax.broadcasted_iota(jnp.int32, (share, HD), 0)
    )
    angles = (position * turn_ref[...]).astype(jnp.float32) * (2.0 * np.pi / 2.0**32)
    cosine = jnp.cos(angles)
    lane = lax.broadcasted_iota(jnp.int32, (share, HD), 1)
    sine = jnp.sin(angles)
    sine = jnp.where(lane < HD // 2, -sine, sine)

    def rotated(ref, offset):
        x = ref[:, pl.ds(pl.multiple_of(offset, 128), HD)].astype(jnp.float32)
        return x * cosine + pltpu.roll(x, HD // 2, 1) * sine

    for which, dst in ((half, q_slots.at[0]), (1 - half, q_other)):
        for head in range(0, half_heads, 2):
            offset = which * (half_heads * HD) + head * HD
            pair = jnp.concatenate(
                [rotated(query_ref, offset), rotated(query_ref, offset + HD)], axis=0
            )
            dst[head * share : (head + 2) * share, :] = pair.astype(jnp.bfloat16)

    def new_rows(which):
        keys = jnp.concatenate(
            [rotated(key_ref, which * half_lanes + g * HD) for g in range(half_kv)], axis=1
        )
        values = value_ref[:, lanes(which, half_lanes)].astype(jnp.float32)
        return keys, values

    other_keys, other_values = new_rows(1 - half)
    new_send[...] = jnp.concatenate([other_keys, other_values], axis=0).astype(jnp.bfloat16)
    own_keys, own_values = new_rows(half)
    live_row = lax.broadcasted_iota(jnp.int32, live_send.shape, 0)
    live_tile = jnp.zeros(live_send.shape, jnp.int32)
    for order in range(span_count):
        live_tile = jnp.where(live_row == order, live_ref[0, flip_bits(near, order)], live_tile)
    live_send[...] = live_tile

    pl.semaphore_wait(barrier, devices - 1)

    def remote(src, dst, ssem, rsem, mask):
        return pltpu.make_async_remote_copy(
            src_ref=src, dst_ref=dst, send_sem=ssem, recv_sem=rsem,
            device_id=target(mask), device_id_type=MESH,
        )

    q_copies = {}
    for mask in range(1, devices):
        sems = (q_ssem.at[mask], q_rsem.at[mask])
        if mask & RELAY:
            q_copies[mask] = remote(q_slots.at[mask - RELAY], q_slots.at[mask], *sems, RELAY)
        else:
            src = q_slots.at[0] if mask % 2 == 0 else q_other
            q_copies[mask] = remote(src, q_slots.at[mask], *sems, mask)
    split = span_devices // 2
    early = [(order, order * span_devices, split) for order in range(1, span_count)]
    late = [(order, begin + split, split) for order, begin, unused in early]
    units = early + late + [(0, 0, span_devices)]

    def direct(begin, count):
        return [mask for mask in range(begin, begin + count) if not mask & RELAY]

    cache_copies = {}

    def swap_cache(order):
        span = flip_bits(near, order)
        for which, (src, dst) in enumerate(((cache_k, k_buf), (cache_v, v_buf))):
            copy = remote(
                src.at[span, :, lanes(1 - half, half_lanes)],
                dst.at[order, pl.ds(slots, slots)],
                cache_ssem.at[order, which], cache_rsem.at[order, which], 1,
            )
            copy.start()
            cache_copies[order, which] = copy

    for unused, begin, count in early:
        for mask in direct(begin, count):
            q_copies[mask].start()
    live_copy = remote(live_send, live_recv, misc_ssem.at[1], misc_rsem.at[1], 1)
    live_copy.start()
    for order in range(1, span_count):
        swap_cache(order)
    for unused, begin, count in late:
        for mask in direct(begin, count):
            q_copies[mask].start()
    for mask in direct(1, span_devices - 1):
        q_copies[mask].start()
    q_copies[RELAY].start()
    new_copy = remote(new_send, new_recv, misc_ssem.at[0], misc_rsem.at[0], 1)
    new_copy.start()
    swap_cache(0)

    stat_lane = lax.broadcasted_iota(jnp.int32, (share, HD), 1)
    group_rows = group_size * share
    o_copies = {mask: [] for mask in range(1, devices)}

    for unused, begin, count in early + late + [(0, 1, span_devices - 1)]:
        for mask in direct(begin, count):
            q_copies[mask].wait_recv()
            q_copies[mask + RELAY].start()

    live_copy.wait_recv()
    for order, first_slot, count in units:
        for mask in range(first_slot, first_slot + count):
            if mask & RELAY:
                q_copies[mask].wait_recv()
        if order == 0:
            new_copy.wait_recv()
        if first_slot == order * span_devices:
            local_copies[2 * order].wait()
            local_copies[2 * order + 1].wait()
            cache_copies[order, 0].wait_recv()
            cache_copies[order, 1].wait_recv()

        column = lax.broadcasted_iota(jnp.int32, (1, slots), 1)
        own_live = live_ref[0, flip_bits(near, order)]
        peer_live = jnp.broadcast_to(live_recv[order : order + 1, 0:1], (1, slots))
        bias = jnp.concatenate(
            [
                jnp.where(column < own_live, 0.0, NEG_FILL),
                jnp.where(column < peer_live, 0.0, NEG_FILL),
            ],
            axis=1,
        )
        row_total = count * group_rows
        if order == 0:
            filler = jnp.zeros((HD - 2 * share, half_lanes), jnp.float32)
            received = new_recv[...].astype(jnp.float32)
            new_keys = jnp.concatenate(
                [own_keys, received[:share], filler], axis=0
            ).astype(jnp.bfloat16)
            new_values = jnp.concatenate(
                [own_values, received[share:], filler], axis=0
            ).astype(jnp.bfloat16)
            pieces = []
            key_column = lax.broadcasted_iota(jnp.int32, (share, HD), 1)
            token_row = lax.broadcasted_iota(jnp.int32, (share, HD), 0)
            key_token = jnp.where(
                key_column < share,
                first_token + key_column,
                flip_bits(me, 1) * share + key_column - share,
            )
            for mask in range(span_devices):
                admitted = (key_column < 2 * share) & (
                    key_token <= flip_bits(me, mask) * share + token_row
                )
                piece = jnp.where(admitted, 0.0, NEG_FILL)
                pieces.extend([piece] * group_size)
            new_bias = jnp.concatenate(pieces, axis=0)

        stats = [jnp.zeros((share, HD), jnp.float32) for unused in range(count)]
        for g in range(half_kv):
            queries = q_slots[
                first_slot : first_slot + count, g * group_rows : (g + 1) * group_rows, :
            ].reshape(row_total, HD)
            head_lanes = slice(g * HD, (g + 1) * HD)
            nt = (((1,), (1,)), ((), ()))
            scores = lax.dot_general(
                queries, k_buf[order, :, head_lanes], nt, preferred_element_type=jnp.float32
            ) + bias
            maxima = jnp.max(scores, axis=1, keepdims=True)
            if order == 0:
                new_scores = lax.dot_general(
                    queries, new_keys[:, head_lanes], nt, preferred_element_type=jnp.float32
                ) + new_bias
                maxima = jnp.maximum(maxima, jnp.max(new_scores, axis=1, keepdims=True))
            maxima = jnp.maximum(maxima, NEG_FLOOR)
            weights = jnp.exp2((scores - maxima) * scale2)
            totals = jnp.sum(weights, axis=1, keepdims=True)
            sums = jnp.dot(
                weights.astype(jnp.bfloat16), v_buf[order, :, head_lanes],
                preferred_element_type=jnp.float32,
            )
            if order == 0:
                new_weights = jnp.exp2((new_scores - maxima) * scale2)
                totals = totals + jnp.sum(new_weights, axis=1, keepdims=True)
                sums = sums + jnp.dot(
                    new_weights.astype(jnp.bfloat16), new_values[:, head_lanes],
                    preferred_element_type=jnp.float32,
                )
            o_send[
                first_slot : first_slot + count, g * group_rows : (g + 1) * group_rows, :
            ] = sums.astype(jnp.bfloat16).reshape(count, group_rows, HD)
            for member in range(count):
                for h in range(group_size):
                    begin = member * group_rows + h * share
                    where = g * group_size + h
                    stats[member] = jnp.where(
                        stat_lane == where, maxima[begin : begin + share], stats[member]
                    )
                    stats[member] = jnp.where(
                        stat_lane == where + HD // 2, totals[begin : begin + share], stats[member]
                    )
        for member in range(count):
            s_send[first_slot + member] = stats[member]
        for member in range(count):
            mask = first_slot + member
            if mask == 0:
                continue
            for src, dst, ssem, rsem in (
                (s_send, s_recv, s_ssem, s_rsem),
                (o_send, o_recv, o_ssem, o_rsem),
            ):
                copy = remote(src.at[mask], dst.at[mask], ssem.at[mask], rsem.at[mask], mask)
                copy.start()
                o_copies[mask].append(copy)

    late_masks = [m for unused, begin, count in late for m in range(begin, begin + count)]
    early_masks = [m for m in range(devices) if m not in late_masks]
    state = {}
    for masks in (early_masks, late_masks):
        for mask in masks:
            for copy in o_copies.get(mask, []):
                copy.wait_recv()
        for parity in range(2):
            members = [m for m in masks if m % 2 == parity]
            stat = [s_send[0] if m == 0 else s_recv[m] for m in members]
            top = functools.reduce(jnp.maximum, stat)
            total = None
            accumulated = [None] * half_heads
            if parity in state:
                old_top, old_total, old_accumulated = state[parity]
                top = jnp.maximum(top, old_top)
                factor = jnp.exp2((old_top - top) * scale2)
                total = old_total * factor
                accumulated = [
                    factor[:, head : head + 1] * old_accumulated[head]
                    for head in range(half_heads)
                ]
            for member, s in zip(members, stat):
                factor = jnp.exp2((s - top) * scale2)
                part = factor * pltpu.roll(s, HD // 2, 1)
                total = part if total is None else total + part
                block = (o_send[0] if member == 0 else o_recv[member]).astype(jnp.float32)
                for head in range(half_heads):
                    term = factor[:, head : head + 1] * block[head * share : (head + 1) * share]
                    accumulated[head] = (
                        term if accumulated[head] is None else accumulated[head] + term
                    )
            state[parity] = (top, total, accumulated)

    for parity in range(2):
        unused_top, total, accumulated = state[parity]
        inverse = 1.0 / total
        which = half if parity == 0 else 1 - half
        out_ref[:, lanes(which, half_heads * HD)] = jnp.concatenate(
            [accumulated[head] * inverse[:, head : head + 1] for head in range(half_heads)],
            axis=1,
        ).astype(jnp.bfloat16)

    result_copies = [copy for pair in o_copies.values() for copy in pair]
    for copy in list(q_copies.values()) + list(cache_copies.values()) + result_copies:
        copy.wait_send()
    new_copy.wait_send()
    live_copy.wait_send()


def fused_device(query_in, key_in, value_in, cache_keys, cache_values, live_slots, span_starts):
    devices = lax.axis_size("kv")
    share = query_in.shape[0]
    spans, slots, kv_width = cache_keys.shape
    kv_heads = kv_width // HD
    group_size = query_in.shape[1] // kv_width
    half_kv = kv_heads // 2
    rows = half_kv * group_size * share
    turns = jnp.concatenate([turn_table(HD)] * 2)[None, :]
    vmem = pl.BlockSpec(memory_space=pltpu.VMEM)
    hbm = pl.BlockSpec(memory_space=pltpu.HBM)
    dma = pltpu.SemaphoreType.DMA
    bf16 = jnp.bfloat16
    return pl.pallas_call(
        functools.partial(attend_kernel, devices, spans, kv_heads, group_size),
        out_shape=jax.ShapeDtypeStruct(query_in.shape, bf16),
        in_specs=[hbm] * 8,
        out_specs=vmem,
        scratch_shapes=[
            pltpu.VMEM(turns.shape, jnp.int32),
            pltpu.VMEM(query_in.shape, bf16),
            pltpu.VMEM(key_in.shape, bf16),
            pltpu.VMEM(value_in.shape, bf16),
            pltpu.SMEM((1, spans), jnp.int32),
            pltpu.SMEM((spans,), jnp.int32),
            dma((6,)),
            pltpu.VMEM((devices, rows, HD), bf16),
            pltpu.VMEM((rows, HD), bf16),
            pltpu.VMEM((spans, 2 * slots, half_kv * HD), bf16),
            pltpu.VMEM((spans, 2 * slots, half_kv * HD), bf16),
            pltpu.VMEM((2 * share, half_kv * HD), bf16),
            pltpu.VMEM((2 * share, half_kv * HD), bf16),
            pltpu.VMEM((8, HD), jnp.int32),
            pltpu.VMEM((8, HD), jnp.int32),
            pltpu.VMEM((devices, rows, HD), bf16),
            pltpu.VMEM((devices, rows, HD), bf16),
            pltpu.VMEM((devices, share, HD), jnp.float32),
            pltpu.VMEM((devices, share, HD), jnp.float32),
            dma((devices,)), dma((devices,)), dma((devices,)), dma((devices,)),
            dma((devices,)), dma((devices,)),
            dma((spans, 2)), dma((spans, 2)), dma((spans, 2)),
            dma((2,)), dma((2,)),
        ],
        compiler_params=pltpu.CompilerParams(
            collective_id=0, has_side_effects=True, vmem_limit_bytes=64 * 2**20 - 65536
        ),
        name="fused_attention",
    )(turns, query_in, key_in, value_in, cache_keys, cache_values, live_slots.T, span_starts)


def is_power(number):
    return number > 0 and number & (number - 1) == 0


def fits_kernel(query_in, key_in, cache_keys, span_starts):
    devices = lax.axis_size("kv")
    spans = span_starts.shape[0]
    kv_heads = key_in.shape[1] // HD
    return (
        is_power(devices)
        and is_power(spans)
        and devices >= 8 * spans and spans >= 2
        and query_in.shape[0] == 8
        and kv_heads % 2 == 0
        and query_in.shape[1] % key_in.shape[1] == 0
        and cache_keys.shape[1] % 128 == 0
        and spans <= 8
        and kv_heads // 2 * (query_in.shape[1] // key_in.shape[1]) <= 64
    )


def one_device(query_in, key_in, value_in, cache_keys, cache_values, live_slots, span_starts):
    arrays = (query_in, key_in, value_in, cache_keys, cache_values, live_slots, span_starts)
    if fits_kernel(query_in, key_in, cache_keys, span_starts):
        return fused_device(*arrays)
    return per_device(*arrays)


def solution(mesh):
    in_specs = (
        P(("groups", "kv"), None),
        P(("groups", "kv"), None),
        P(("groups", "kv"), None),
        P("groups", "kv", None),
        P("groups", "kv", None),
        P("groups", "kv"),
        P("groups"),
    )
    out_specs = P(("groups", "kv"), None)
    return jax.shard_map(
        one_device, mesh=mesh, in_specs=in_specs, out_specs=out_specs, check_vma=False
    )
```

```python
import functools
import math

import jax
import jax.numpy as jnp
import numpy as np
from jax import lax
from jax.experimental import pallas as pl
from jax.experimental.pallas import tpu as pltpu
from jax.sharding import PartitionSpec as P

HD = 128


NEG_FILL = -1e30
NEG_FLOOR = -1e29
MESH = pl.DeviceIdType.MESH


def turn_table(head_size):
    half_size = head_size // 2
    frequency = 500000.0 ** (-np.arange(half_size) * 2.0 / head_size)
    turn_counts = np.floor(frequency / (2.0 * np.pi) * 2.0**32 + 0.5).astype(np.int64) % 2**32
    turn_counts = np.where(turn_counts >= 2**31, turn_counts - 2**32, turn_counts)
    return jnp.asarray(turn_counts.astype(np.int32))


def rotate_pairs(values, positions):
    half_size = values.shape[-1] // 2
    phases = positions[:, None] * turn_table(values.shape[-1])[None, :]
    angles = phases.astype(jnp.float32) * (2.0 * np.pi / 2.0**32)
    cosine = jnp.cos(angles)[:, None, :]
    sine_table = jnp.sin(angles)[:, None, :]
    first_half = values[..., :half_size]
    second_half = values[..., half_size:]
    return jnp.concatenate(
        [
            first_half * cosine - second_half * sine_table,
            second_half * cosine + first_half * sine_table,
        ],
        axis=-1,
    )


def partial_block(query_rows, block_keys, block_values, allowed):
    row_count = query_rows.shape[0]
    kv_heads = block_keys.shape[1]
    head_size = block_keys.shape[2]
    grouped = query_rows.reshape(row_count, kv_heads, -1, head_size)
    scores = jnp.einsum(
        "rkgd,skd->kgrs", grouped, block_keys, preferred_element_type=jnp.float32
    ) * head_size ** (-0.5)
    scores = jnp.where(allowed, scores, NEG_FILL)
    maxima = jnp.max(scores, axis=-1)
    weights = jnp.where(allowed, jnp.exp(scores - maxima[..., None]), 0.0)
    totals = jnp.sum(weights, axis=-1)
    weighted_sum = jnp.einsum(
        "kgrs,skd->rkgd",
        weights.astype(jnp.bfloat16),
        block_values,
        preferred_element_type=jnp.float32,
    )
    return (
        jnp.transpose(maxima, (2, 0, 1)).reshape(row_count, -1),
        jnp.transpose(totals, (2, 0, 1)).reshape(row_count, -1),
        weighted_sum.reshape(row_count, -1),
    )


def fold_pair(first_terms, second_terms):
    first_max, first_total, first_sum = first_terms
    second_max, second_total, second_sum = second_terms
    joint_max = jnp.maximum(first_max, second_max)
    first_factor = jnp.exp(first_max - joint_max)
    second_factor = jnp.exp(second_max - joint_max)
    row_count, head_count = joint_max.shape
    weighted = (
        first_sum.reshape(row_count, head_count, -1) * first_factor[..., None]
        + second_sum.reshape(row_count, head_count, -1) * second_factor[..., None]
    )
    return (
        joint_max,
        first_total * first_factor + second_total * second_factor,
        weighted.reshape(row_count, -1),
    )


def rescale(local_max, local_total, local_sum, global_max):
    factor = jnp.exp(local_max - global_max)
    row_count, head_count = factor.shape
    scaled_sum = (local_sum.reshape(row_count, head_count, -1) * factor[..., None]).reshape(
        row_count, -1
    )
    return (local_total * factor, scaled_sum)


def normalize(combined):
    unused_max, totals, sums = combined
    row_count, head_count = totals.shape
    return (
        (sums.reshape(row_count, head_count, -1) / totals[..., None])
        .reshape(row_count, -1)
        .astype(jnp.bfloat16)
    )


def attend_own(query_rows, row_start, keys_new, values_new, span_len):
    query_count = query_rows.shape[0]
    rows_each = min(query_count, span_len)
    blocks = max(query_count // span_len, 1)
    pieces = []
    for block_index in range(blocks):
        first_row = row_start + block_index * rows_each
        key_start = first_row // span_len * span_len
        block_keys = lax.dynamic_slice_in_dim(keys_new, key_start, span_len, 0)
        block_values = lax.dynamic_slice_in_dim(values_new, key_start, span_len, 0)
        allowed = (
            first_row - key_start + jnp.arange(rows_each)[:, None] >= jnp.arange(span_len)[None, :]
        )
        block_rows = query_rows[block_index * rows_each : (block_index + 1) * rows_each]
        pieces.append(partial_block(block_rows, block_keys, block_values, allowed))
    return tuple(
        (
            jnp.concatenate([block_terms[member] for block_terms in pieces], axis=0)
            for member in range(3)
        )
    )


def per_device(query_in, key_in, value_in, cache_keys, cache_values, live_slots, span_starts):
    devices = lax.axis_size("kv")
    device_index = lax.axis_index("kv")
    share_rows = query_in.shape[0]
    token_count = share_rows * devices
    span_count = span_starts.shape[0]
    span_len = token_count // span_count
    head_size = HD
    head_count = query_in.shape[1] // head_size
    kv_heads = key_in.shape[1] // head_size
    row_start = device_index * share_rows
    positions = (span_starts[:, None] + jnp.arange(span_len, dtype=jnp.int32)[None, :]).reshape(
        token_count
    )
    full_query, full_key, full_value = (
        lax.all_gather(query_in, "kv", axis=0, tiled=True),
        lax.all_gather(key_in, "kv", axis=0, tiled=True),
        lax.all_gather(value_in, "kv", axis=0, tiled=True),
    )
    queries = rotate_pairs(
        full_query.astype(jnp.float32).reshape(token_count, head_count, head_size), positions
    ).astype(jnp.bfloat16)
    keys_new = rotate_pairs(
        full_key.astype(jnp.float32).reshape(token_count, kv_heads, head_size), positions
    ).astype(jnp.bfloat16)
    values_new = full_value.reshape(token_count, kv_heads, head_size)
    slot_count = cache_keys.shape[1]
    slot_index = jnp.arange(slot_count)
    partials = []
    for span_index in range(span_count):
        query_rows = queries[span_index * span_len : (span_index + 1) * span_len]
        allowed = (slot_index < live_slots[span_index, 0])[None, :]
        block_keys = cache_keys[span_index].reshape(slot_count, kv_heads, head_size)
        block_values = cache_values[span_index].reshape(slot_count, kv_heads, head_size)
        partials.append(partial_block(query_rows, block_keys, block_values, allowed))
    local_max, local_total, local_sum = tuple(
        (
            jnp.concatenate([block_terms[member] for block_terms in partials], axis=0)
            for member in range(3)
        )
    )
    global_max = lax.pmax(local_max, "kv")
    scaled_total, scaled_sum = rescale(local_max, local_total, local_sum, global_max)
    total_all, sum_all = lax.psum((scaled_total, scaled_sum), "kv")
    own_terms = attend_own(queries, 0, keys_new, values_new, span_len)
    attended = normalize(fold_pair((global_max, total_all, sum_all), own_terms))
    return lax.dynamic_slice_in_dim(attended, row_start, share_rows, 0)


RELAY = 2


def flip_bits(index, mask):
    result = index
    bit = 1
    while bit <= mask:
        if mask & bit:
            result = result + bit * (1 - 2 * lax.rem(lax.div(index, bit), 2))
        bit *= 2
    return result


def attend_kernel(
    devices, span_count, kv_heads, group_size,
    turn_hbm, query_hbm, key_hbm, value_hbm, cache_k, cache_v, live_hbm, start_hbm, out_ref,
    turn_ref, query_ref, key_ref, value_ref, live_ref, start_ref, in_sem,
    q_slots, q_other, k_buf, v_buf, new_send, new_recv, live_send, live_recv,
    o_send, o_recv, s_send, s_recv,
    q_ssem, q_rsem, o_ssem, o_rsem, s_ssem, s_rsem, cache_ssem, cache_rsem, local_sem,
    misc_ssem, misc_rsem,
):
    share = query_hbm.shape[0]
    slots = cache_k.shape[1]
    half_kv = kv_heads // 2
    half_heads = half_kv * group_size
    half_lanes = half_kv * HD
    span_devices = devices // span_count
    span_len = share * span_devices
    scale2 = HD ** (-0.5) * math.log2(math.e)

    me = lax.axis_index("kv")
    half = lax.rem(me, 2)
    near = lax.div(me, span_devices)

    def target(mask):
        return {"kv": flip_bits(me, mask)}

    def lanes(which, width):
        return pl.ds(pl.multiple_of(which * width, 128), width)

    barrier = pltpu.get_barrier_semaphore()
    for mask in range(1, devices):
        pl.semaphore_signal(barrier, inc=1, device_id=target(mask), device_id_type=MESH)

    operand_copies = []
    for index, (src, dst) in enumerate(
        (
            (start_hbm, start_ref), (turn_hbm, turn_ref), (query_hbm, query_ref),
            (key_hbm, key_ref), (value_hbm, value_ref), (live_hbm, live_ref),
        )
    ):
        copy = pltpu.make_async_copy(src, dst, in_sem.at[index])
        copy.start()
        operand_copies.append(copy)

    local_copies = []
    for order in range(span_count):
        span = flip_bits(near, order)
        for which, (src, dst) in enumerate(((cache_k, k_buf), (cache_v, v_buf))):
            copy = pltpu.make_async_copy(
                src.at[span, :, lanes(half, half_lanes)],
                dst.at[order, pl.ds(0, slots)],
                local_sem.at[order, which],
            )
            copy.start()
            local_copies.append(copy)

    for copy in operand_copies:
        copy.wait()
    first_token = me * share
    position = (
        start_ref[near]
        + (first_token - near * span_len)
        + lax.broadcasted_iota(jnp.int32, (share, HD), 0)
    )
    angles = (position * turn_ref[...]).astype(jnp.float32) * (2.0 * np.pi / 2.0**32)
    cosine = jnp.cos(angles)
    lane = lax.broadcasted_iota(jnp.int32, (share, HD), 1)
    sine = jnp.sin(angles)
    sine = jnp.where(lane < HD // 2, -sine, sine)

    def rotated(ref, offset):
        x = ref[:, pl.ds(pl.multiple_of(offset, 128), HD)].astype(jnp.float32)
        return x * cosine + pltpu.roll(x, HD // 2, 1) * sine

    for which, dst in ((half, q_slots.at[0]), (1 - half, q_other)):
        for head in range(0, half_heads, 2):
            offset = which * (half_heads * HD) + head * HD
            pair = jnp.concatenate(
                [rotated(query_ref, offset), rotated(query_ref, offset + HD)], axis=0
            )
            dst[head * share : (head + 2) * share, :] = pair.astype(jnp.bfloat16)

    def new_rows(which):
        keys = jnp.concatenate(
            [rotated(key_ref, which * half_lanes + g * HD) for g in range(half_kv)], axis=1
        )
        values = value_ref[:, lanes(which, half_lanes)].astype(jnp.float32)
        return keys, values

    other_keys, other_values = new_rows(1 - half)
    new_send[...] = jnp.concatenate([other_keys, other_values], axis=0).astype(jnp.bfloat16)
    own_keys, own_values = new_rows(half)
    live_row = lax.broadcasted_iota(jnp.int32, live_send.shape, 0)
    live_tile = jnp.zeros(live_send.shape, jnp.int32)
    for order in range(span_count):
        live_tile = jnp.where(live_row == order, live_ref[0, flip_bits(near, order)], live_tile)
    live_send[...] = live_tile

    pl.semaphore_wait(barrier, devices - 1)

    def remote(src, dst, ssem, rsem, mask):
        return pltpu.make_async_remote_copy(
            src_ref=src, dst_ref=dst, send_sem=ssem, recv_sem=rsem,
            device_id=target(mask), device_id_type=MESH,
        )

    q_copies = {}
    for mask in range(1, devices):
        sems = (q_ssem.at[mask], q_rsem.at[mask])
        if mask & RELAY:
            q_copies[mask] = remote(q_slots.at[mask - RELAY], q_slots.at[mask], *sems, RELAY)
        else:
            src = q_slots.at[0] if mask % 2 == 0 else q_other
            q_copies[mask] = remote(src, q_slots.at[mask], *sems, mask)
    split = span_devices // 2
    early = [(order, order * span_devices, split) for order in range(1, span_count)]
    late = [(order, begin + split, split) for order, begin, unused in early]
    units = early + [(0, 0, span_devices)] + late

    def direct(begin, count):
        return [mask for mask in range(begin, begin + count) if not mask & RELAY]

    cache_copies = {}

    def swap_cache(order):
        span = flip_bits(near, order)
        for which, (src, dst) in enumerate(((cache_k, k_buf), (cache_v, v_buf))):
            copy = remote(
                src.at[span, :, lanes(1 - half, half_lanes)],
                dst.at[order, pl.ds(slots, slots)],
                cache_ssem.at[order, which], cache_rsem.at[order, which], 1,
            )
            copy.start()
            cache_copies[order, which] = copy

    for unused, begin, count in early:
        for mask in direct(begin, count):
            q_copies[mask].start()
    live_copy = remote(live_send, live_recv, misc_ssem.at[1], misc_rsem.at[1], 1)
    live_copy.start()
    for order in range(1, span_count):
        swap_cache(order)
    for unused, begin, count in late:
        for mask in direct(begin, count):
            q_copies[mask].start()
    for mask in direct(1, span_devices - 1):
        q_copies[mask].start()
    q_copies[RELAY].start()
    new_copy = remote(new_send, new_recv, misc_ssem.at[0], misc_rsem.at[0], 1)
    new_copy.start()
    swap_cache(0)

    stat_lane = lax.broadcasted_iota(jnp.int32, (share, HD), 1)
    group_rows = group_size * share
    o_copies = {mask: [] for mask in range(1, devices)}

    for unused, begin, count in early + late + [(0, 1, span_devices - 1)]:
        for mask in direct(begin, count):
            q_copies[mask].wait_recv()
            q_copies[mask + RELAY].start()

    live_copy.wait_recv()
    for order, first_slot, count in units:
        for mask in range(first_slot, first_slot + count):
            if mask & RELAY:
                q_copies[mask].wait_recv()
        if order == 0:
            new_copy.wait_recv()
        if first_slot == order * span_devices:
            local_copies[2 * order].wait()
            local_copies[2 * order + 1].wait()
            cache_copies[order, 0].wait_recv()
            cache_copies[order, 1].wait_recv()

        column = lax.broadcasted_iota(jnp.int32, (1, slots), 1)
        own_live = live_ref[0, flip_bits(near, order)]
        peer_live = jnp.broadcast_to(live_recv[order : order + 1, 0:1], (1, slots))
        bias = jnp.concatenate(
            [
                jnp.where(column < own_live, 0.0, NEG_FILL),
                jnp.where(column < peer_live, 0.0, NEG_FILL),
            ],
            axis=1,
        )
        row_total = count * group_rows
        if order == 0:
            filler = jnp.zeros((HD - 2 * share, half_lanes), jnp.float32)
            received = new_recv[...].astype(jnp.float32)
            new_keys = jnp.concatenate(
                [own_keys, received[:share], filler], axis=0
            ).astype(jnp.bfloat16)
            new_values = jnp.concatenate(
                [own_values, received[share:], filler], axis=0
            ).astype(jnp.bfloat16)
            pieces = []
            key_column = lax.broadcasted_iota(jnp.int32, (share, HD), 1)
            token_row = lax.broadcasted_iota(jnp.int32, (share, HD), 0)
            key_token = jnp.where(
                key_column < share,
                first_token + key_column,
                flip_bits(me, 1) * share + key_column - share,
            )
            for mask in range(span_devices):
                admitted = (key_column < 2 * share) & (
                    key_token <= flip_bits(me, mask) * share + token_row
                )
                piece = jnp.where(admitted, 0.0, NEG_FILL)
                pieces.extend([piece] * group_size)
            new_bias = jnp.concatenate(pieces, axis=0)

        stats = [jnp.zeros((share, HD), jnp.float32) for unused in range(count)]
        for g in range(half_kv):
            queries = q_slots[
                first_slot : first_slot + count, g * group_rows : (g + 1) * group_rows, :
            ].reshape(row_total, HD)
            head_lanes = slice(g * HD, (g + 1) * HD)
            nt = (((1,), (1,)), ((), ()))
            scores = lax.dot_general(
                queries, k_buf[order, :, head_lanes], nt, preferred_element_type=jnp.float32
            ) + bias
            maxima = jnp.max(scores, axis=1, keepdims=True)
            if order == 0:
                new_scores = lax.dot_general(
                    queries, new_keys[:, head_lanes], nt, preferred_element_type=jnp.float32
                ) + new_bias
                maxima = jnp.maximum(maxima, jnp.max(new_scores, axis=1, keepdims=True))
            maxima = jnp.maximum(maxima, NEG_FLOOR)
            weights = jnp.exp2((scores - maxima) * scale2)
            totals = jnp.sum(weights, axis=1, keepdims=True)
            sums = jnp.dot(
                weights.astype(jnp.bfloat16), v_buf[order, :, head_lanes],
                preferred_element_type=jnp.float32,
            )
            if order == 0:
                new_weights = jnp.exp2((new_scores - maxima) * scale2)
                totals = totals + jnp.sum(new_weights, axis=1, keepdims=True)
                sums = sums + jnp.dot(
                    new_weights.astype(jnp.bfloat16), new_values[:, head_lanes],
                    preferred_element_type=jnp.float32,
                )
            o_send[
                first_slot : first_slot + count, g * group_rows : (g + 1) * group_rows, :
            ] = sums.astype(jnp.bfloat16).reshape(count, group_rows, HD)
            for mask in range(max(first_slot, 1), first_slot + count):
                rows = pl.ds(g * group_rows, group_rows)
                copy = remote(
                    o_send.at[mask, rows], o_recv.at[mask, rows],
                    o_ssem.at[mask, g], o_rsem.at[mask, g], mask,
                )
                copy.start()
                o_copies[mask].append(copy)
            for member in range(count):
                for h in range(group_size):
                    begin = member * group_rows + h * share
                    where = g * group_size + h
                    stats[member] = jnp.where(
                        stat_lane == where, maxima[begin : begin + share], stats[member]
                    )
                    stats[member] = jnp.where(
                        stat_lane == where + HD // 2, totals[begin : begin + share], stats[member]
                    )
        for member in range(count):
            s_send[first_slot + member] = stats[member]
        for member in range(count):
            mask = first_slot + member
            if mask == 0:
                continue
            copy = remote(
                s_send.at[mask], s_recv.at[mask], s_ssem.at[mask], s_rsem.at[mask], mask
            )
            copy.start()
            o_copies[mask].append(copy)

    late_masks = [m for unused, begin, count in late for m in range(begin, begin + count)]
    early_masks = [m for m in range(devices) if m not in late_masks]
    state = {}
    for masks in (early_masks, late_masks):
        for mask in masks:
            for copy in o_copies.get(mask, []):
                copy.wait_recv()
        for parity in range(2):
            members = [m for m in masks if m % 2 == parity]
            stat = [s_send[0] if m == 0 else s_recv[m] for m in members]
            top = functools.reduce(jnp.maximum, stat)
            total = None
            accumulated = [None] * half_heads
            if parity in state:
                old_top, old_total, old_accumulated = state[parity]
                top = jnp.maximum(top, old_top)
                factor = jnp.exp2((old_top - top) * scale2)
                total = old_total * factor
                accumulated = [
                    factor[:, head : head + 1] * old_accumulated[head]
                    for head in range(half_heads)
                ]
            for member, s in zip(members, stat):
                factor = jnp.exp2((s - top) * scale2)
                part = factor * pltpu.roll(s, HD // 2, 1)
                total = part if total is None else total + part
                block = (o_send[0] if member == 0 else o_recv[member]).astype(jnp.float32)
                for head in range(half_heads):
                    term = factor[:, head : head + 1] * block[head * share : (head + 1) * share]
                    accumulated[head] = (
                        term if accumulated[head] is None else accumulated[head] + term
                    )
            state[parity] = (top, total, accumulated)

    for parity in range(2):
        unused_top, total, accumulated = state[parity]
        inverse = 1.0 / total
        which = half if parity == 0 else 1 - half
        out_ref[:, lanes(which, half_heads * HD)] = jnp.concatenate(
            [accumulated[head] * inverse[:, head : head + 1] for head in range(half_heads)],
            axis=1,
        ).astype(jnp.bfloat16)

    result_copies = [copy for pair in o_copies.values() for copy in pair]
    for copy in list(q_copies.values()) + list(cache_copies.values()) + result_copies:
        copy.wait_send()
    new_copy.wait_send()
    live_copy.wait_send()


def fused_device(query_in, key_in, value_in, cache_keys, cache_values, live_slots, span_starts):
    devices = lax.axis_size("kv")
    share = query_in.shape[0]
    spans, slots, kv_width = cache_keys.shape
    kv_heads = kv_width // HD
    group_size = query_in.shape[1] // kv_width
    half_kv = kv_heads // 2
    rows = half_kv * group_size * share
    turns = jnp.concatenate([turn_table(HD)] * 2)[None, :]
    vmem = pl.BlockSpec(memory_space=pltpu.VMEM)
    hbm = pl.BlockSpec(memory_space=pltpu.HBM)
    dma = pltpu.SemaphoreType.DMA
    bf16 = jnp.bfloat16
    return pl.pallas_call(
        functools.partial(attend_kernel, devices, spans, kv_heads, group_size),
        out_shape=jax.ShapeDtypeStruct(query_in.shape, bf16),
        in_specs=[hbm] * 8,
        out_specs=vmem,
        scratch_shapes=[
            pltpu.VMEM(turns.shape, jnp.int32),
            pltpu.VMEM(query_in.shape, bf16),
            pltpu.VMEM(key_in.shape, bf16),
            pltpu.VMEM(value_in.shape, bf16),
            pltpu.SMEM((1, spans), jnp.int32),
            pltpu.SMEM((spans,), jnp.int32),
            dma((6,)),
            pltpu.VMEM((devices, rows, HD), bf16),
            pltpu.VMEM((rows, HD), bf16),
            pltpu.VMEM((spans, 2 * slots, half_kv * HD), bf16),
            pltpu.VMEM((spans, 2 * slots, half_kv * HD), bf16),
            pltpu.VMEM((2 * share, half_kv * HD), bf16),
            pltpu.VMEM((2 * share, half_kv * HD), bf16),
            pltpu.VMEM((8, HD), jnp.int32),
            pltpu.VMEM((8, HD), jnp.int32),
            pltpu.VMEM((devices, rows, HD), bf16),
            pltpu.VMEM((devices, rows, HD), bf16),
            pltpu.VMEM((devices, share, HD), jnp.float32),
            pltpu.VMEM((devices, share, HD), jnp.float32),
            dma((devices,)), dma((devices,)), dma((devices, half_kv)), dma((devices, half_kv)),
            dma((devices,)), dma((devices,)),
            dma((spans, 2)), dma((spans, 2)), dma((spans, 2)),
            dma((2,)), dma((2,)),
        ],
        compiler_params=pltpu.CompilerParams(
            collective_id=0, has_side_effects=True, vmem_limit_bytes=64 * 2**20 - 65536
        ),
        name="fused_attention",
    )(turns, query_in, key_in, value_in, cache_keys, cache_values, live_slots.T, span_starts)


def is_power(number):
    return number > 0 and number & (number - 1) == 0


def fits_kernel(query_in, key_in, cache_keys, span_starts):
    devices = lax.axis_size("kv")
    spans = span_starts.shape[0]
    kv_heads = key_in.shape[1] // HD
    return (
        is_power(devices)
        and is_power(spans)
        and devices >= 8 * spans and spans >= 2
        and query_in.shape[0] == 8
        and kv_heads % 2 == 0
        and query_in.shape[1] % key_in.shape[1] == 0
        and cache_keys.shape[1] % 128 == 0
        and spans <= 8
        and kv_heads // 2 * (query_in.shape[1] // key_in.shape[1]) <= 64
    )


def one_device(query_in, key_in, value_in, cache_keys, cache_values, live_slots, span_starts):
    arrays = (query_in, key_in, value_in, cache_keys, cache_values, live_slots, span_starts)
    if fits_kernel(query_in, key_in, cache_keys, span_starts):
        return fused_device(*arrays)
    return per_device(*arrays)


def solution(mesh):
    in_specs = (
        P(("groups", "kv"), None),
        P(("groups", "kv"), None),
        P(("groups", "kv"), None),
        P("groups", "kv", None),
        P("groups", "kv", None),
        P("groups", "kv"),
        P("groups"),
    )
    out_specs = P(("groups", "kv"), None)
    return jax.shard_map(
        one_device, mesh=mesh, in_specs=in_specs, out_specs=out_specs, check_vma=False
    )
```

```python
import functools
import math

import jax
import jax.numpy as jnp
import numpy as np
from jax import lax
from jax.experimental import pallas as pl
from jax.experimental.pallas import tpu as pltpu
from jax.sharding import PartitionSpec as P

HD = 128


NEG_FILL = -1e30
NEG_FLOOR = -1e29
MESH = pl.DeviceIdType.MESH


def turn_table(head_size):
    half_size = head_size // 2
    frequency = 500000.0 ** (-np.arange(half_size) * 2.0 / head_size)
    turn_counts = np.floor(frequency / (2.0 * np.pi) * 2.0**32 + 0.5).astype(np.int64) % 2**32
    turn_counts = np.where(turn_counts >= 2**31, turn_counts - 2**32, turn_counts)
    return jnp.asarray(turn_counts.astype(np.int32))


def rotate_pairs(values, positions):
    half_size = values.shape[-1] // 2
    phases = positions[:, None] * turn_table(values.shape[-1])[None, :]
    angles = phases.astype(jnp.float32) * (2.0 * np.pi / 2.0**32)
    cosine = jnp.cos(angles)[:, None, :]
    sine_table = jnp.sin(angles)[:, None, :]
    first_half = values[..., :half_size]
    second_half = values[..., half_size:]
    return jnp.concatenate(
        [
            first_half * cosine - second_half * sine_table,
            second_half * cosine + first_half * sine_table,
        ],
        axis=-1,
    )


def partial_block(query_rows, block_keys, block_values, allowed):
    row_count = query_rows.shape[0]
    kv_heads = block_keys.shape[1]
    head_size = block_keys.shape[2]
    grouped = query_rows.reshape(row_count, kv_heads, -1, head_size)
    scores = jnp.einsum(
        "rkgd,skd->kgrs", grouped, block_keys, preferred_element_type=jnp.float32
    ) * head_size ** (-0.5)
    scores = jnp.where(allowed, scores, NEG_FILL)
    maxima = jnp.max(scores, axis=-1)
    weights = jnp.where(allowed, jnp.exp(scores - maxima[..., None]), 0.0)
    totals = jnp.sum(weights, axis=-1)
    weighted_sum = jnp.einsum(
        "kgrs,skd->rkgd",
        weights.astype(jnp.bfloat16),
        block_values,
        preferred_element_type=jnp.float32,
    )
    return (
        jnp.transpose(maxima, (2, 0, 1)).reshape(row_count, -1),
        jnp.transpose(totals, (2, 0, 1)).reshape(row_count, -1),
        weighted_sum.reshape(row_count, -1),
    )


def fold_pair(first_terms, second_terms):
    first_max, first_total, first_sum = first_terms
    second_max, second_total, second_sum = second_terms
    joint_max = jnp.maximum(first_max, second_max)
    first_factor = jnp.exp(first_max - joint_max)
    second_factor = jnp.exp(second_max - joint_max)
    row_count, head_count = joint_max.shape
    weighted = (
        first_sum.reshape(row_count, head_count, -1) * first_factor[..., None]
        + second_sum.reshape(row_count, head_count, -1) * second_factor[..., None]
    )
    return (
        joint_max,
        first_total * first_factor + second_total * second_factor,
        weighted.reshape(row_count, -1),
    )


def rescale(local_max, local_total, local_sum, global_max):
    factor = jnp.exp(local_max - global_max)
    row_count, head_count = factor.shape
    scaled_sum = (local_sum.reshape(row_count, head_count, -1) * factor[..., None]).reshape(
        row_count, -1
    )
    return (local_total * factor, scaled_sum)


def normalize(combined):
    unused_max, totals, sums = combined
    row_count, head_count = totals.shape
    return (
        (sums.reshape(row_count, head_count, -1) / totals[..., None])
        .reshape(row_count, -1)
        .astype(jnp.bfloat16)
    )


def attend_own(query_rows, row_start, keys_new, values_new, span_len):
    query_count = query_rows.shape[0]
    rows_each = min(query_count, span_len)
    blocks = max(query_count // span_len, 1)
    pieces = []
    for block_index in range(blocks):
        first_row = row_start + block_index * rows_each
        key_start = first_row // span_len * span_len
        block_keys = lax.dynamic_slice_in_dim(keys_new, key_start, span_len, 0)
        block_values = lax.dynamic_slice_in_dim(values_new, key_start, span_len, 0)
        allowed = (
            first_row - key_start + jnp.arange(rows_each)[:, None] >= jnp.arange(span_len)[None, :]
        )
        block_rows = query_rows[block_index * rows_each : (block_index + 1) * rows_each]
        pieces.append(partial_block(block_rows, block_keys, block_values, allowed))
    return tuple(
        (
            jnp.concatenate([block_terms[member] for block_terms in pieces], axis=0)
            for member in range(3)
        )
    )


def per_device(query_in, key_in, value_in, cache_keys, cache_values, live_slots, span_starts):
    devices = lax.axis_size("kv")
    device_index = lax.axis_index("kv")
    share_rows = query_in.shape[0]
    token_count = share_rows * devices
    span_count = span_starts.shape[0]
    span_len = token_count // span_count
    head_size = HD
    head_count = query_in.shape[1] // head_size
    kv_heads = key_in.shape[1] // head_size
    row_start = device_index * share_rows
    positions = (span_starts[:, None] + jnp.arange(span_len, dtype=jnp.int32)[None, :]).reshape(
        token_count
    )
    full_query, full_key, full_value = (
        lax.all_gather(query_in, "kv", axis=0, tiled=True),
        lax.all_gather(key_in, "kv", axis=0, tiled=True),
        lax.all_gather(value_in, "kv", axis=0, tiled=True),
    )
    queries = rotate_pairs(
        full_query.astype(jnp.float32).reshape(token_count, head_count, head_size), positions
    ).astype(jnp.bfloat16)
    keys_new = rotate_pairs(
        full_key.astype(jnp.float32).reshape(token_count, kv_heads, head_size), positions
    ).astype(jnp.bfloat16)
    values_new = full_value.reshape(token_count, kv_heads, head_size)
    slot_count = cache_keys.shape[1]
    slot_index = jnp.arange(slot_count)
    partials = []
    for span_index in range(span_count):
        query_rows = queries[span_index * span_len : (span_index + 1) * span_len]
        allowed = (slot_index < live_slots[span_index, 0])[None, :]
        block_keys = cache_keys[span_index].reshape(slot_count, kv_heads, head_size)
        block_values = cache_values[span_index].reshape(slot_count, kv_heads, head_size)
        partials.append(partial_block(query_rows, block_keys, block_values, allowed))
    local_max, local_total, local_sum = tuple(
        (
            jnp.concatenate([block_terms[member] for block_terms in partials], axis=0)
            for member in range(3)
        )
    )
    global_max = lax.pmax(local_max, "kv")
    scaled_total, scaled_sum = rescale(local_max, local_total, local_sum, global_max)
    total_all, sum_all = lax.psum((scaled_total, scaled_sum), "kv")
    own_terms = attend_own(queries, 0, keys_new, values_new, span_len)
    attended = normalize(fold_pair((global_max, total_all, sum_all), own_terms))
    return lax.dynamic_slice_in_dim(attended, row_start, share_rows, 0)


RELAY = 2


def flip_bits(index, mask):
    result = index
    bit = 1
    while bit <= mask:
        if mask & bit:
            result = result + bit * (1 - 2 * lax.rem(lax.div(index, bit), 2))
        bit *= 2
    return result


def attend_kernel(
    devices, span_count, kv_heads, group_size,
    turn_hbm, query_hbm, key_hbm, value_hbm, cache_k, cache_v, live_hbm, start_hbm, out_ref,
    turn_ref, query_ref, key_ref, value_ref, live_ref, start_ref, in_sem,
    q_slots, q_other, k_buf, v_buf, new_send, new_recv, live_send, live_recv,
    o_send, o_recv,
    q_ssem, q_rsem, o_ssem, o_rsem, cache_ssem, cache_rsem, local_sem,
    misc_ssem, misc_rsem,
):
    share = query_hbm.shape[0]
    slots = cache_k.shape[1]
    half_kv = kv_heads // 2
    half_heads = half_kv * group_size
    half_lanes = half_kv * HD
    stat_begin = half_heads * share
    span_devices = devices // span_count
    span_len = share * span_devices
    scale2 = HD ** (-0.5) * math.log2(math.e)

    me = lax.axis_index("kv")
    half = lax.rem(me, 2)
    near = lax.div(me, span_devices)

    def target(mask):
        return {"kv": flip_bits(me, mask)}

    def lanes(which, width):
        return pl.ds(pl.multiple_of(which * width, 128), width)

    barrier = pltpu.get_barrier_semaphore()
    for mask in range(1, devices):
        pl.semaphore_signal(barrier, inc=1, device_id=target(mask), device_id_type=MESH)

    operand_copies = []
    for index, (src, dst) in enumerate(
        (
            (start_hbm, start_ref), (turn_hbm, turn_ref), (query_hbm, query_ref),
            (key_hbm, key_ref), (value_hbm, value_ref), (live_hbm, live_ref),
        )
    ):
        copy = pltpu.make_async_copy(src, dst, in_sem.at[index])
        copy.start()
        operand_copies.append(copy)

    local_copies = []
    for order in range(span_count):
        span = flip_bits(near, order)
        for which, (src, dst) in enumerate(((cache_k, k_buf), (cache_v, v_buf))):
            copy = pltpu.make_async_copy(
                src.at[span, :, lanes(half, half_lanes)],
                dst.at[order, pl.ds(0, slots)],
                local_sem.at[order, which],
            )
            copy.start()
            local_copies.append(copy)

    for copy in operand_copies:
        copy.wait()
    first_token = me * share
    position = (
        start_ref[near]
        + (first_token - near * span_len)
        + lax.broadcasted_iota(jnp.int32, (share, HD), 0)
    )
    angles = (position * turn_ref[...]).astype(jnp.float32) * (2.0 * np.pi / 2.0**32)
    cosine = jnp.cos(angles)
    lane = lax.broadcasted_iota(jnp.int32, (share, HD), 1)
    sine = jnp.sin(angles)
    sine = jnp.where(lane < HD // 2, -sine, sine)

    def rotated(ref, offset):
        x = ref[:, pl.ds(pl.multiple_of(offset, 128), HD)].astype(jnp.float32)
        return x * cosine + pltpu.roll(x, HD // 2, 1) * sine

    for which, dst in ((half, q_slots.at[0]), (1 - half, q_other)):
        for head in range(0, half_heads, 2):
            offset = which * (half_heads * HD) + head * HD
            pair = jnp.concatenate(
                [rotated(query_ref, offset), rotated(query_ref, offset + HD)], axis=0
            )
            dst[head * share : (head + 2) * share, :] = pair.astype(jnp.bfloat16)

    def new_rows(which):
        keys = jnp.concatenate(
            [rotated(key_ref, which * half_lanes + g * HD) for g in range(half_kv)], axis=1
        )
        values = value_ref[:, lanes(which, half_lanes)].astype(jnp.float32)
        return keys, values

    other_keys, other_values = new_rows(1 - half)
    new_send[...] = jnp.concatenate([other_keys, other_values], axis=0).astype(jnp.bfloat16)
    own_keys, own_values = new_rows(half)
    live_row = lax.broadcasted_iota(jnp.int32, live_send.shape, 0)
    live_tile = jnp.zeros(live_send.shape, jnp.int32)
    for order in range(span_count):
        live_tile = jnp.where(live_row == order, live_ref[0, flip_bits(near, order)], live_tile)
    live_send[...] = live_tile

    pl.semaphore_wait(barrier, devices - 1)

    def remote(src, dst, ssem, rsem, mask):
        return pltpu.make_async_remote_copy(
            src_ref=src, dst_ref=dst, send_sem=ssem, recv_sem=rsem,
            device_id=target(mask), device_id_type=MESH,
        )

    q_copies = {}
    for mask in range(1, devices):
        sems = (q_ssem.at[mask], q_rsem.at[mask])
        if mask & RELAY:
            q_copies[mask] = remote(q_slots.at[mask - RELAY], q_slots.at[mask], *sems, RELAY)
        else:
            src = q_slots.at[0] if mask % 2 == 0 else q_other
            q_copies[mask] = remote(src, q_slots.at[mask], *sems, mask)
    split = span_devices // 2
    early = [(order, order * span_devices, split) for order in range(1, span_count)]
    late = [(order, begin + split, split) for order, begin, unused in early]
    units = early + [(0, 0, span_devices)] + late

    def direct(begin, count):
        return [mask for mask in range(begin, begin + count) if not mask & RELAY]

    cache_copies = {}

    def swap_cache(order):
        span = flip_bits(near, order)
        for which, (src, dst) in enumerate(((cache_k, k_buf), (cache_v, v_buf))):
            copy = remote(
                src.at[span, :, lanes(1 - half, half_lanes)],
                dst.at[order, pl.ds(slots, slots)],
                cache_ssem.at[order, which], cache_rsem.at[order, which], 1,
            )
            copy.start()
            cache_copies[order, which] = copy

    for unused, begin, count in early:
        for mask in direct(begin, count):
            q_copies[mask].start()
    live_copy = remote(live_send, live_recv, misc_ssem.at[1], misc_rsem.at[1], 1)
    live_copy.start()
    for order in range(1, span_count):
        swap_cache(order)
    for unused, begin, count in late:
        for mask in direct(begin, count):
            q_copies[mask].start()
    for mask in direct(1, span_devices - 1):
        q_copies[mask].start()
    q_copies[RELAY].start()
    new_copy = remote(new_send, new_recv, misc_ssem.at[0], misc_rsem.at[0], 1)
    new_copy.start()
    swap_cache(0)

    stat_lane = lax.broadcasted_iota(jnp.int32, (share, HD), 1)
    group_rows = group_size * share
    o_copies = {mask: [] for mask in range(1, devices)}

    for unused, begin, count in early + late + [(0, 1, span_devices - 1)]:
        for mask in direct(begin, count):
            q_copies[mask].wait_recv()
            q_copies[mask + RELAY].start()

    live_copy.wait_recv()
    for order, first_slot, count in units:
        for mask in range(first_slot, first_slot + count):
            if mask & RELAY:
                q_copies[mask].wait_recv()
        if order == 0:
            new_copy.wait_recv()
        if first_slot == order * span_devices:
            local_copies[2 * order].wait()
            local_copies[2 * order + 1].wait()
            cache_copies[order, 0].wait_recv()
            cache_copies[order, 1].wait_recv()

        column = lax.broadcasted_iota(jnp.int32, (1, slots), 1)
        own_live = live_ref[0, flip_bits(near, order)]
        peer_live = jnp.broadcast_to(live_recv[order : order + 1, 0:1], (1, slots))
        bias = jnp.concatenate(
            [
                jnp.where(column < own_live, 0.0, NEG_FILL),
                jnp.where(column < peer_live, 0.0, NEG_FILL),
            ],
            axis=1,
        )
        row_total = count * group_rows
        if order == 0:
            filler = jnp.zeros((HD - 2 * share, half_lanes), jnp.float32)
            received = new_recv[...].astype(jnp.float32)
            new_keys = jnp.concatenate(
                [own_keys, received[:share], filler], axis=0
            ).astype(jnp.bfloat16)
            new_values = jnp.concatenate(
                [own_values, received[share:], filler], axis=0
            ).astype(jnp.bfloat16)
            pieces = []
            key_column = lax.broadcasted_iota(jnp.int32, (share, HD), 1)
            token_row = lax.broadcasted_iota(jnp.int32, (share, HD), 0)
            key_token = jnp.where(
                key_column < share,
                first_token + key_column,
                flip_bits(me, 1) * share + key_column - share,
            )
            for mask in range(span_devices):
                admitted = (key_column < 2 * share) & (
                    key_token <= flip_bits(me, mask) * share + token_row
                )
                piece = jnp.where(admitted, 0.0, NEG_FILL)
                pieces.extend([piece] * group_size)
            new_bias = jnp.concatenate(pieces, axis=0)

        stats = [jnp.zeros((share, HD), jnp.float32) for unused in range(count)]
        for g in range(half_kv):
            queries = q_slots[
                first_slot : first_slot + count, g * group_rows : (g + 1) * group_rows, :
            ].reshape(row_total, HD)
            head_lanes = slice(g * HD, (g + 1) * HD)
            nt = (((1,), (1,)), ((), ()))
            scores = lax.dot_general(
                queries, k_buf[order, :, head_lanes], nt, preferred_element_type=jnp.float32
            ) + bias
            maxima = jnp.max(scores, axis=1, keepdims=True)
            if order == 0:
                new_scores = lax.dot_general(
                    queries, new_keys[:, head_lanes], nt, preferred_element_type=jnp.float32
                ) + new_bias
                maxima = jnp.maximum(maxima, jnp.max(new_scores, axis=1, keepdims=True))
            maxima = jnp.maximum(maxima, NEG_FLOOR)
            weights = jnp.exp2((scores - maxima) * scale2)
            totals = jnp.sum(weights, axis=1, keepdims=True)
            sums = jnp.dot(
                weights.astype(jnp.bfloat16), v_buf[order, :, head_lanes],
                preferred_element_type=jnp.float32,
            )
            if order == 0:
                new_weights = jnp.exp2((new_scores - maxima) * scale2)
                totals = totals + jnp.sum(new_weights, axis=1, keepdims=True)
                sums = sums + jnp.dot(
                    new_weights.astype(jnp.bfloat16), new_values[:, head_lanes],
                    preferred_element_type=jnp.float32,
                )
            o_send[
                first_slot : first_slot + count, g * group_rows : (g + 1) * group_rows, :
            ] = sums.astype(jnp.bfloat16).reshape(count, group_rows, HD)
            for member in range(count):
                for h in range(group_size):
                    begin = member * group_rows + h * share
                    where = g * group_size + h
                    stats[member] = jnp.where(
                        stat_lane == where, maxima[begin : begin + share], stats[member]
                    )
                    stats[member] = jnp.where(
                        stat_lane == where + HD // 2, totals[begin : begin + share], stats[member]
                    )
        for member in range(count):
            value = stats[member]
            high = value.astype(jnp.bfloat16).astype(jnp.float32)
            middle = (value - high).astype(jnp.bfloat16).astype(jnp.float32)
            low = pltpu.roll(value - high - middle, half_heads, 1)
            o_send[first_slot + member, stat_begin : stat_begin + 2 * share, :] = (
                jnp.concatenate([high, middle + low], axis=0).astype(jnp.bfloat16)
            )
        for member in range(count):
            mask = first_slot + member
            if mask == 0:
                continue
            for src, dst, ssem, rsem in (
                (o_send, o_recv, o_ssem, o_rsem),
            ):
                copy = remote(src.at[mask], dst.at[mask], ssem.at[mask], rsem.at[mask], mask)
                copy.start()
                o_copies[mask].append(copy)

    late_masks = [m for unused, begin, count in late for m in range(begin, begin + count)]
    early_masks = [m for m in range(devices) if m not in late_masks]
    state = {}
    for masks in (early_masks, late_masks):
        for mask in masks:
            for copy in o_copies.get(mask, []):
                copy.wait_recv()
        for parity in range(2):
            members = [m for m in masks if m % 2 == parity]
            stat = []
            for m in members:
                packed = (o_send if m == 0 else o_recv)[
                    m, stat_begin : stat_begin + 2 * share, :
                ].astype(jnp.float32)
                rest = packed[share:]
                stat.append(packed[:share] + (rest + pltpu.roll(rest, HD - half_heads, 1)))
            top = functools.reduce(jnp.maximum, stat)
            total = None
            accumulated = [None] * half_heads
            if parity in state:
                old_top, old_total, old_accumulated = state[parity]
                top = jnp.maximum(top, old_top)
                factor = jnp.exp2((old_top - top) * scale2)
                total = old_total * factor
                accumulated = [
                    factor[:, head : head + 1] * old_accumulated[head]
                    for head in range(half_heads)
                ]
            for member, s in zip(members, stat):
                factor = jnp.exp2((s - top) * scale2)
                part = factor * pltpu.roll(s, HD // 2, 1)
                total = part if total is None else total + part
                block = (o_send[0] if member == 0 else o_recv[member]).astype(jnp.float32)
                for head in range(half_heads):
                    term = factor[:, head : head + 1] * block[head * share : (head + 1) * share]
                    accumulated[head] = (
                        term if accumulated[head] is None else accumulated[head] + term
                    )
            state[parity] = (top, total, accumulated)

    for parity in range(2):
        unused_top, total, accumulated = state[parity]
        inverse = 1.0 / total
        which = half if parity == 0 else 1 - half
        out_ref[:, lanes(which, half_heads * HD)] = jnp.concatenate(
            [accumulated[head] * inverse[:, head : head + 1] for head in range(half_heads)],
            axis=1,
        ).astype(jnp.bfloat16)

    result_copies = [copy for pair in o_copies.values() for copy in pair]
    for copy in list(q_copies.values()) + list(cache_copies.values()) + result_copies:
        copy.wait_send()
    new_copy.wait_send()
    live_copy.wait_send()


def fused_device(query_in, key_in, value_in, cache_keys, cache_values, live_slots, span_starts):
    devices = lax.axis_size("kv")
    share = query_in.shape[0]
    spans, slots, kv_width = cache_keys.shape
    kv_heads = kv_width // HD
    group_size = query_in.shape[1] // kv_width
    half_kv = kv_heads // 2
    rows = half_kv * group_size * share
    turns = jnp.concatenate([turn_table(HD)] * 2)[None, :]
    vmem = pl.BlockSpec(memory_space=pltpu.VMEM)
    hbm = pl.BlockSpec(memory_space=pltpu.HBM)
    dma = pltpu.SemaphoreType.DMA
    bf16 = jnp.bfloat16
    return pl.pallas_call(
        functools.partial(attend_kernel, devices, spans, kv_heads, group_size),
        out_shape=jax.ShapeDtypeStruct(query_in.shape, bf16),
        in_specs=[hbm] * 8,
        out_specs=vmem,
        scratch_shapes=[
            pltpu.VMEM(turns.shape, jnp.int32),
            pltpu.VMEM(query_in.shape, bf16),
            pltpu.VMEM(key_in.shape, bf16),
            pltpu.VMEM(value_in.shape, bf16),
            pltpu.SMEM((1, spans), jnp.int32),
            pltpu.SMEM((spans,), jnp.int32),
            dma((6,)),
            pltpu.VMEM((devices, rows, HD), bf16),
            pltpu.VMEM((rows, HD), bf16),
            pltpu.VMEM((spans, 2 * slots, half_kv * HD), bf16),
            pltpu.VMEM((spans, 2 * slots, half_kv * HD), bf16),
            pltpu.VMEM((2 * share, half_kv * HD), bf16),
            pltpu.VMEM((2 * share, half_kv * HD), bf16),
            pltpu.VMEM((8, HD), jnp.int32),
            pltpu.VMEM((8, HD), jnp.int32),
            pltpu.VMEM((devices, rows + 2 * share, HD), bf16),
            pltpu.VMEM((devices, rows + 2 * share, HD), bf16),
            dma((devices,)), dma((devices,)), dma((devices,)), dma((devices,)),
            dma((spans, 2)), dma((spans, 2)), dma((spans, 2)),
            dma((2,)), dma((2,)),
        ],
        compiler_params=pltpu.CompilerParams(
            collective_id=0, has_side_effects=True, vmem_limit_bytes=64 * 2**20 - 65536
        ),
        name="fused_attention",
    )(turns, query_in, key_in, value_in, cache_keys, cache_values, live_slots.T, span_starts)


def is_power(number):
    return number > 0 and number & (number - 1) == 0


def fits_kernel(query_in, key_in, cache_keys, span_starts):
    devices = lax.axis_size("kv")
    spans = span_starts.shape[0]
    kv_heads = key_in.shape[1] // HD
    return (
        is_power(devices)
        and is_power(spans)
        and devices >= 8 * spans and spans >= 2
        and query_in.shape[0] == 8
        and kv_heads % 2 == 0
        and query_in.shape[1] % key_in.shape[1] == 0
        and cache_keys.shape[1] % 128 == 0
        and spans <= 8
        and kv_heads // 2 * (query_in.shape[1] // key_in.shape[1]) <= 16
    )


def one_device(query_in, key_in, value_in, cache_keys, cache_values, live_slots, span_starts):
    arrays = (query_in, key_in, value_in, cache_keys, cache_values, live_slots, span_starts)
    if fits_kernel(query_in, key_in, cache_keys, span_starts):
        return fused_device(*arrays)
    return per_device(*arrays)


def solution(mesh):
    in_specs = (
        P(("groups", "kv"), None),
        P(("groups", "kv"), None),
        P(("groups", "kv"), None),
        P("groups", "kv", None),
        P("groups", "kv", None),
        P("groups", "kv"),
        P("groups"),
    )
    out_specs = P(("groups", "kv"), None)
    return jax.shard_map(
        one_device, mesh=mesh, in_specs=in_specs, out_specs=out_specs, check_vma=False
    )
```
